128 devices in a mesh: row: 4 (over x), col: 32 (over y, z, core).
Axes of the slice: x: 4, y: 4, z: 4, core: 2. Of those that a mesh axis runs over, the one named last changes fastest.
Arguments:
- features: bfloat16 [32768, 128], P(('row', 'col')), may hold values from -6 to 6
- weight: bfloat16 [128, 256], replicated, may hold values from -0.5 to 0.5
- bias_vector: float32 [256], replicated, may hold values from -3 to 3
- adjacency: bfloat16 [4, 32, 128, 128, 128], P('row', 'col'), may hold values from -0.078125 to 0.078125
- tile_rows: int32 [4, 32, 128], P('row', 'col'), may hold values from 0 to 63, as said below
- tile_cols: int32 [4, 32, 128], P('row', 'col'), may hold values from 0 to 7
- tile_count: int32 [4, 32], P('row', 'col'), may hold values from 32 to 128, as said below
- cotangent: bfloat16 [32768, 256], P(('row', 'col')), may hold values from -6 to 6
Outputs:
- activations: bfloat16 [32768, 256], P(('row', 'col'))
- grad_features: bfloat16 [32768, 128], P(('row', 'col'))
- grad_weight: float32 [128, 256], replicated
- grad_bias: float32 [256], replicated
The draws below stay inside these ranges and needn't reach their ends.
Inputs may be any that keep to these rules, and one draw needn't show every extreme that they name: Within one grid cell no two slots name the same pair of tile_rows and tile_cols. On each grid cell the live tiles are the first tile_count slots; at least one cell has all 128 slots live.
All inputs are finite; a program needn't handle non-finite values.
Results may differ from the reference program's by a relative error of at most 0.0075.
Values may be sent and summed in bfloat16 or wider, within the bound.
No kernel may reach another device: no remote copies, remote signals or barrier semaphores. Data moves between devices by JAX's collectives and lax.ppermute only.
A program may use at most 128 MiB of HBM per device.

```python
import jax
import jax.numpy as jnp
from jax import lax

BLOCK = 128
F_IN = 128
HID = 256
BPD = 2
TILES_DEV = 128
NODES = 32768
ROW_BLOCKS = 64
COL_BLOCKS = 8
N_ROW = 4
N_COL = 32


def tile_spots(key):
    cells = N_ROW * N_COL
    cell_keys = jax.random.split(key, cells)

    def pick(cell_key):
        return jax.random.permutation(cell_key, ROW_BLOCKS * COL_BLOCKS)[:TILES_DEV]
    spots = jax.vmap(pick)(cell_keys).astype(jnp.int32)
    return spots.reshape(N_ROW, N_COL, TILES_DEV)


def draw_tile_rows(key, part):
    spots = tile_spots(key)
    return (spots // COL_BLOCKS).astype(jnp.int32)


def draw_tile_cols(key, part):
    spots = tile_spots(key)
    return (spots % COL_BLOCKS).astype(jnp.int32)


def draw_tile_count(key, part):
    key = jax.random.fold_in(key, 7)
    count_key, spot_key = jax.random.split(key)
    counts = jax.random.randint(count_key, (N_ROW * N_COL,), TILES_DEV // 4, TILES_DEV + 1, dtype=jnp.int32)
    spot = jax.random.randint(spot_key, (), 0, N_ROW * N_COL, dtype=jnp.int32)
    places = jnp.arange(N_ROW * N_COL, dtype=jnp.int32)
    counts = jnp.where(places == spot, jnp.int32(TILES_DEV), counts)
    return counts.reshape(N_ROW, N_COL).astype(jnp.int32)


def steps_of(key, extent, pieces, least, high):
    def one(axis_at, blocks):
        heights = jax.random.uniform(jax.random.fold_in(jax.random.fold_in(key, 6), axis_at), (blocks,), jnp.float32, least / len(pieces), high / len(pieces))
        return jnp.repeat(jnp.exp(heights), extent[axis_at] // blocks).reshape((-1,) + (1,) * (len(extent) - axis_at - 1))

    level = one(*pieces[0])
    for cut in pieces[1:]:
        level = level * one(*cut)
    return level


def centred(rng, dims, width, bound, pieces=(), kind=jnp.bfloat16):
    entries = jax.random.normal(rng, dims, jnp.float32) * width
    if len(pieces) > 0:
        entries = steps_of(rng, dims, pieces, -0.22, 0.18) * entries
    return jnp.clip(entries, min=-bound, max=bound).astype(kind)


def setup_inputs(seed: int = 0) -> dict:
    splits = jax.random.split(jax.random.key(seed), 9)
    return {
        "features": centred(splits[0], (NODES, F_IN), 1.0, 6.0, ((0, 128),)),
        "weight": centred(splits[1], (F_IN, HID), F_IN ** -0.5, 0.5),
        "bias_vector": centred(splits[2], (HID,), 0.5, 3.0, (), jnp.float32),
        "adjacency": centred(splits[3], (N_ROW, N_COL, TILES_DEV, BLOCK, BLOCK), (TILES_DEV * BLOCK * 5 // (8 * BPD)) ** -0.5, 0.078125, ((0, 4), (1, 32))),
        "tile_rows": draw_tile_rows(jax.random.fold_in(splits[8], 71), 0),
        "tile_cols": draw_tile_cols(jax.random.fold_in(splits[8], 71), 0),
        "tile_count": draw_tile_count(jax.random.fold_in(splits[8], 71), 0),
        "cotangent": centred(splits[7], (NODES, HID), 1.0, 6.0, ((0, 128),)),
    }


def forward_tiles(adjacency, tile_rows, tile_cols, live_count, column_feats, row_count):
    gathered = jnp.take(column_feats, tile_cols, axis=0).astype(jnp.float32)
    products = jnp.einsum("tij,tjh->tih", adjacency.astype(jnp.float32), gathered)
    live_mask = (jnp.arange(adjacency.shape[0], dtype=jnp.int32) < live_count).astype(jnp.float32)
    products = products * live_mask[:, None, None]
    return jax.ops.segment_sum(products, tile_rows, num_segments=row_count)


def backward_tiles(adjacency, tile_rows, tile_cols, live_count, row_grads, col_count):
    gathered = jnp.take(row_grads, tile_rows, axis=0).astype(jnp.float32)
    products = jnp.einsum("tji,tjh->tih", adjacency.astype(jnp.float32), gathered)
    live_mask = (jnp.arange(adjacency.shape[0], dtype=jnp.int32) < live_count).astype(jnp.float32)
    products = products * live_mask[:, None, None]
    return jax.ops.segment_sum(products, tile_cols, num_segments=col_count)


def reference(features, weight, bias_vector, adjacency, tile_rows, tile_cols, tile_count, cotangent):
    projected = jnp.dot(features, weight, preferred_element_type=jnp.float32).astype(jnp.bfloat16)
    z_grid = projected.reshape(N_ROW, N_COL, BPD * BLOCK, HID)
    devices = jnp.arange(N_ROW * N_COL, dtype=jnp.int32)

    def forward_step(running, device):
        grid_row = device // N_COL
        grid_col = device % N_COL
        column_feats = lax.dynamic_index_in_dim(z_grid, grid_col, 1, keepdims=False)
        column_feats = column_feats.reshape(COL_BLOCKS, BLOCK, HID)
        part = forward_tiles(adjacency[grid_row, grid_col], tile_rows[grid_row, grid_col],
                             tile_cols[grid_row, grid_col], tile_count[grid_row, grid_col],
                             column_feats, ROW_BLOCKS)
        return running.at[grid_row].add(part), None

    start_rows = jnp.zeros((N_ROW, ROW_BLOCKS, BLOCK, HID), jnp.float32)
    summed, _ = lax.scan(forward_step, start_rows, devices)
    pre = summed.reshape(NODES, HID) + bias_vector
    sigmoid_value = jax.nn.sigmoid(pre)
    activations = (pre * sigmoid_value).astype(jnp.bfloat16)
    slope = sigmoid_value * (1.0 + pre * (1.0 - sigmoid_value))
    node_grad = (cotangent.astype(jnp.float32) * slope).astype(jnp.bfloat16)
    grad_grid = node_grad.reshape(N_ROW, ROW_BLOCKS, BLOCK, HID)

    def backward_step(running, device):
        grid_row = device // N_COL
        grid_col = device % N_COL
        part = backward_tiles(adjacency[grid_row, grid_col], tile_rows[grid_row, grid_col],
                              tile_cols[grid_row, grid_col], tile_count[grid_row, grid_col],
                              grad_grid[grid_row], COL_BLOCKS)
        part = part.reshape(N_ROW, BPD * BLOCK, HID)
        return running.at[:, grid_col].add(part), None

    start_cols = jnp.zeros((N_ROW, N_COL, BPD * BLOCK, HID), jnp.float32)
    proj_sum, _ = lax.scan(backward_step, start_cols, devices)
    proj_grad = proj_sum.reshape(NODES, HID).astype(jnp.bfloat16)
    grad_weight = jnp.dot(features.T, proj_grad, preferred_element_type=jnp.float32)
    grad_bias = jnp.sum(node_grad.astype(jnp.float32), axis=0)
    grad_features = jnp.dot(proj_grad, weight.T, preferred_element_type=jnp.float32).astype(jnp.bfloat16)
    return activations, grad_features, grad_weight, grad_bias
```

```python
import functools

import jax
import jax.numpy as jnp
from jax import lax
from jax.experimental import pallas as pl
from jax.experimental.pallas import tpu as pltpu
from jax.sharding import PartitionSpec as P

F32 = jnp.float32
BF16 = jnp.bfloat16
B = 128
VMEM = pl.BlockSpec(memory_space=pltpu.VMEM)
SMEM = pl.BlockSpec(memory_space=pltpu.SMEM)
TAIL = 272
UNROLL = 8


def at(y, z, core):
    return (y * 4 + z) * 2 + core


def col_shift(first, d):
    pairs = []
    for y in range(4):
        for z in range(4):
            for core in range(2):
                along_z = (core == 0) == first
                to = at(y, (z + d) % 4, core) if along_z else at((y + d) % 4, z, core)
                pairs.append((at(y, z, core), to))
    return pairs


def core_swap():
    return [(c, c ^ 1) for c in range(32)]


def row_shift(d):
    return [(r, (r + d) % 4) for r in range(4)]


def call(kernel, outs, n_smem, n_vmem, scratch=(), flops=0, nbytes=0):
    return pl.pallas_call(
        kernel,
        out_shape=outs,
        in_specs=[SMEM] * n_smem + [VMEM] * n_vmem,
        out_specs=jax.tree.map(lambda _: VMEM, outs),
        scratch_shapes=list(scratch),
        compiler_params=pltpu.CompilerParams(vmem_limit_bytes=24 * 2**20),
        cost_estimate=pl.CostEstimate(flops=flops, bytes_accessed=nbytes, transcendentals=0),
    )


def sds(rows, cols=B, dtype=BF16):
    return jax.ShapeDtypeStruct((rows, cols), dtype)


def forward_tiles(pos, src, x0, x1, x2, x3, adj, own, other, acc, xs):
    for k, x in enumerate((x0, x1, x2, x3)):
        xs[2 * k] = x[0:B]
        xs[2 * k + 1] = x[B : 2 * B]

    def clear(i, _):
        acc[i] = jnp.zeros((B, B), F32)
        return 0

    lax.fori_loop(0, 64, clear, 0)

    def body(g, _):
        parts = []
        for u in range(UNROLL):
            s = g * UNROLL + u
            parts.append(jnp.dot(adj[s], xs[src[s]], preferred_element_type=F32))
        for u in range(UNROLL):
            p = pos[g * UNROLL + u]
            acc[p] += parts[u]
        return 0

    lax.fori_loop(0, 128 // UNROLL, body, 0)

    def store(i, _):
        rows = pl.ds(pl.multiple_of(i * B, B), B)
        own[rows] = acc[i]
        other[rows] = acc[32 + i].astype(BF16)
        return 0

    lax.fori_loop(0, 32, store, 0)


def core_sum(own, got, m0, m1, m2, m3):
    m0[...] = own[0:1024] + got[0:1024].astype(F32)
    for k, m in ((1, m1), (2, m2), (3, m3)):
        rows = pl.ds(k * 1024, 1024)
        m[...] = (own[rows] + got[rows].astype(F32)).astype(BF16)


def first_sum(m0, r1, r2, r3, s0, s1, s2, s3):
    for k, s in enumerate((s0, s1, s2, s3)):
        rows = pl.ds(k * 256, 256)
        total = m0[rows] + (r1[rows].astype(F32) + r2[rows].astype(F32) + r3[rows].astype(F32))
        s[...] = total.astype(s.dtype)


def put_tail(msg, base, wg, bg):
    msg[pl.ds(base, 256)] = wg.astype(msg.dtype)
    if msg.dtype == F32:
        msg[pl.ds(base + 256, 16)] = jnp.concatenate([bg, jnp.zeros((14, B), F32)])
    else:
        high = bg.astype(BF16).astype(F32)
        low = bg - high
        block = jnp.concatenate([high, low, jnp.zeros((12, B), F32)])
        msg[pl.ds(base + 256, 16)] = block.astype(BF16)


def get_tail(msg, base):
    wg = msg[pl.ds(base, 256)].astype(F32)
    block = msg[pl.ds(base + 256, 16)].astype(F32)
    return wg, block[0:2] + block[2:4]


def local(s0, r1, r2, r3, weight, bias, cot, act, msg):
    y = s0[...] + (r1[...].astype(F32) + r2[...].astype(F32) + r3[...].astype(F32))
    y_high = y.astype(BF16)
    y_low = (y - y_high.astype(F32)).astype(BF16)
    w = weight[...]
    summed = jnp.dot(y_high, w, preferred_element_type=F32) + jnp.dot(
        y_low, w, preferred_element_type=F32
    )
    pre = summed + bias[...]
    sig = jax.nn.sigmoid(pre)
    act[...] = (pre * sig).astype(BF16)
    slope = sig * (1.0 + pre * (1.0 - sig))
    grad = (cot[...].astype(F32) * slope).astype(BF16)
    g = lax.dot_general(w, grad, (((1,), (1,)), ((), ())), preferred_element_type=F32)
    g = g.astype(BF16)
    msg[0:B] = g[:, 0:B]
    msg[B : 2 * B] = g[:, B : 2 * B]
    over_nodes = (((0,), (0,)), ((), ()))
    wg = lax.dot_general(y_high, grad, over_nodes, preferred_element_type=F32)
    wg += lax.dot_general(y_low, grad, over_nodes, preferred_element_type=F32)
    bg = jnp.sum(grad.astype(F32), axis=0, keepdims=True)
    put_tail(
        msg,
        256,
        jnp.concatenate([wg[:, 0:B], wg[:, B : 2 * B]]),
        jnp.concatenate([bg[:, 0:B], bg[:, B : 2 * B]]),
    )


def second_join(m0, r1, r2, r3, msg):
    wg, bg = get_tail(m0, 256)
    for r in (r1, r2, r3):
        wg_r, bg_r = get_tail(r, 256)
        wg += wg_r
        bg += bg_r
    for k, r in enumerate((m0, r3, r2, r1)):
        msg[pl.ds(k * 256, 256)] = r[0:256]
    put_tail(msg, 1024, wg, bg)


def backward_tiles(pos, src, *refs):
    pieces, (adj, m0, m1, m2, m3, acc, gs) = refs[:8], refs[8:]

    def load(i, _):
        rows = pl.ds(pl.multiple_of(i * B, B), B)
        for k, piece in enumerate(pieces):
            gs[k * 8 + i] = piece[rows]
        return 0

    lax.fori_loop(0, 8, load, 0)
    gs[64] = jnp.zeros((B, B), BF16)
    acc[...] = jnp.zeros((8, B, B), F32)

    def body(g, _):
        parts = []
        for u in range(UNROLL):
            s = g * UNROLL + u
            parts.append(jnp.dot(gs[pos[s]], adj[s], preferred_element_type=F32))
        for u in range(UNROLL):
            q = src[g * UNROLL + u]
            acc[q] += parts[u]
        return 0

    lax.fori_loop(0, 128 // UNROLL, body, 0)
    wg, bg = get_tail(pieces[0], 1024)
    for piece in pieces[1:]:
        wg_r, bg_r = get_tail(piece, 1024)
        wg += wg_r
        bg += bg_r
    for k, m in enumerate((m0, m1, m2, m3)):
        m[0:B] = acc[2 * k].astype(m.dtype)
        m[B : 2 * B] = acc[2 * k + 1].astype(m.dtype)
        put_tail(m, 256, wg, bg)


def last_sum(m0, r1, r2, r3, feat, wgrad, bgrad):
    for k in range(2):
        rows = pl.ds(k * B, B)
        total = m0[rows] + (r1[rows].astype(F32) + r2[rows].astype(F32) + r3[rows].astype(F32))
        feat[rows] = total.T.astype(BF16)
    wg, block = m0[pl.ds(256, 256)], m0[pl.ds(512, 16)]
    bg = block[0:2]
    for r in (r1, r2, r3):
        wg_r, bg_r = get_tail(r, 256)
        wg += wg_r
        bg += bg_r
    wgrad[:, 0:B] = wg[0:B]
    wgrad[:, B : 2 * B] = wg[B : 2 * B]
    bgrad[:, 0:B] = bg[0:1]
    bgrad[:, B : 2 * B] = bg[1:2]


def on_device(
    features, weight, bias_vector, adjacency, tile_rows, tile_cols, tile_count, cotangent
):
    r = lax.axis_index("row")
    c = lax.axis_index("col")
    core, z, y = c % 2, (c // 2) % 4, c // 8

    owner, sub = tile_rows[0, 0] // 2, tile_rows[0, 0] % 2
    core_to, z_to, y_to = owner % 2, (owner // 2) % 4, owner // 8
    dz, dy = (z_to - z) % 4, (y_to - y) % 4
    first = jnp.where(core_to == 0, dz, dy)
    second = jnp.where(core_to == 0, dy, dz)
    half = (core_to != core).astype(jnp.int32)
    pos = ((half * 4 + first) * 4 + second) * 2 + sub
    live = jnp.arange(pos.shape[0], dtype=jnp.int32) < tile_count[0, 0]
    pos = jnp.where(live, pos, 64)
    src = ((tile_cols[0, 0] // 2 - r) % 4) * 2 + tile_cols[0, 0] % 2
    adj = adjacency[0, 0]

    x1, x2, x3 = (lax.ppermute(features, "row", row_shift(d)) for d in (1, 2, 3))
    own, other = call(
        forward_tiles,
        (sds(4096, dtype=F32), sds(4096)),
        2,
        5,
        [pltpu.VMEM((65, B, B), F32), pltpu.VMEM((8, B, B), BF16)],
        flops=2 * 128 * B**3,
        nbytes=8 * 2**20,
    )(pos, src, features, x3, x2, x1, adj)
    got = lax.ppermute(other, "col", core_swap())
    m0, *ms = call(core_sum, (sds(1024, dtype=F32), sds(1024), sds(1024), sds(1024)), 0, 2)(own, got)
    rs = [lax.ppermute(m, "col", col_shift(True, d + 1)) for d, m in enumerate(ms)]
    s0, *ss = call(first_sum, (sds(256, dtype=F32), sds(256), sds(256), sds(256)), 0, 4)(m0, *rs)
    rs = [lax.ppermute(s, "col", col_shift(False, d + 1)) for d, s in enumerate(ss)]
    act, msg = call(local, (sds(256, 256), sds(256 + TAIL)), 0, 7)(
        s0, *rs, weight, bias_vector.reshape(1, 256), cotangent
    )
    rs = [lax.ppermute(msg, "col", col_shift(False, d)) for d in (1, 2, 3)]
    msg = call(second_join, sds(1024 + TAIL), 0, 4)(msg, *rs)
    rs = [lax.ppermute(msg, "col", col_shift(True, d)) for d in (1, 2, 3)]
    mine = (msg, rs[2], rs[1], rs[0])
    theirs = [lax.ppermute(m, "col", core_swap()) for m in mine]
    x_out = (sds(256 + TAIL, dtype=F32),) + (sds(256 + TAIL),) * 3
    m0, *ms = call(
        backward_tiles,
        x_out,
        2,
        9,
        [pltpu.VMEM((8, B, B), F32), pltpu.VMEM((65, B, B), BF16)],
        flops=2 * 128 * B**3,
        nbytes=8 * 2**20,
    )(pos, src, *mine, *theirs, adj)
    rs = [lax.ppermute(m, "row", row_shift(d + 1)) for d, m in enumerate(ms)]
    feat, wgrad, bgrad = call(
        last_sum, (sds(256, 128), sds(128, 256, F32), sds(1, 256, F32)), 0, 4
    )(m0, *rs)
    return (act, feat, wgrad, bgrad.reshape(256))


def solution(mesh):
    placed = (
        P(("row", "col"), None),
        P(),
        P(),
        P("row", "col", None, None, None),
        P("row", "col", None),
        P("row", "col", None),
        P("row", "col"),
        P(("row", "col"), None),
    )
    return jax.shard_map(
        on_device,
        mesh=mesh,
        in_specs=placed,
        out_specs=(P(("row", "col"), None), P(("row", "col"), None), P(), P()),
        check_vma=False,
    )
```

```python
import functools

import jax
import jax.numpy as jnp
from jax import lax
from jax.experimental import pallas as pl
from jax.experimental.pallas import tpu as pltpu
from jax.sharding import PartitionSpec as P

F32 = jnp.float32
BF16 = jnp.bfloat16
B = 128
VMEM = pl.BlockSpec(memory_space=pltpu.VMEM)
SMEM = pl.BlockSpec(memory_space=pltpu.SMEM)
ANY = pl.BlockSpec(memory_space=pl.ANY)
TAIL = 272
UNROLL = 16
LEAD = 2**24
WIDTH = 144
TAB = 384
BACKWARD_TAB = 512


def at(y, z, core):
    return (y * 4 + z) * 2 + core


def col_shift(first, d):
    pairs = []
    for y in range(4):
        for z in range(4):
            for core in range(2):
                along_z = (core == 0) == first
                to = at(y, (z + d) % 4, core) if along_z else at((y + d) % 4, z, core)
                pairs.append((at(y, z, core), to))
    return pairs


def core_swap():
    return [(c, c ^ 1) for c in range(32)]


def row_shift(d):
    return [(r, (r + d) % 4) for r in range(4)]


def call(kernel, outs, ins, scratch=(), tiles=0, nbytes=0):
    return pl.pallas_call(
        kernel,
        out_shape=outs,
        in_specs=ins,
        out_specs=jax.tree.map(lambda _: VMEM, outs),
        scratch_shapes=list(scratch),
        compiler_params=pltpu.CompilerParams(vmem_limit_bytes=24 * 2**20),
        cost_estimate=pl.CostEstimate(
            flops=2 * tiles * B**3, bytes_accessed=nbytes + tiles * 2**16, transcendentals=0
        ),
    )


def sds(rows, cols=B, dtype=BF16):
    return jax.ShapeDtypeStruct((rows, cols), dtype)


def permute(arrays, axis, pairs):
    arrays = lax.optimization_barrier(tuple(arrays))
    return [lax.ppermute(a, axis, p) for a, p in zip(arrays, pairs)]


ORDER = (2, 1, 3)


def live_slots(count, live):
    slot = lax.broadcasted_iota(jnp.int32, (1, 128), 1)
    live[...] = (slot < count[0, 0]).astype(jnp.int32)


def sort_tiles(rows, cols, live, forward_tab, backward_tab):
    r, c = lax.axis_index("row"), lax.axis_index("col")
    core, z, y = c % 2, (c // 2) % 4, c // 8
    rows, cols = rows[...], cols[...]
    owner, sub = rows // 2, rows % 2
    core_to, z_to, y_to = owner % 2, (owner // 2) % 4, owner // 8
    dz, dy = (z_to - z + 4) % 4, (y_to - y + 4) % 4
    first = jnp.where(core_to == 0, dz, dy)
    second = jnp.where(core_to == 0, dy, dz)
    pos = (first * 4 + second) * 2 + sub
    half = (core_to != core).astype(jnp.int32)
    ahead = (cols // 2 - r + 4) % 4
    slot = lax.broadcasted_iota(jnp.int32, (1, 128), 1)

    def table(key, keys, take, to, pad, width):
        key = jnp.where(live[...] == 1, key, keys)
        is_key = [jnp.where(key == k, 1.0, 0.0) for k in range(keys)]
        is_key = jnp.concatenate(is_key + [jnp.zeros((8 - keys, 128), F32)]).astype(BF16)
        low = lax.broadcasted_iota(jnp.int32, (128, 128), 0)
        high = lax.broadcasted_iota(jnp.int32, (128, 128), 1)
        before = jnp.where(low < high, 1.0, 0.0).astype(BF16)
        rank = jnp.dot(is_key, before, preferred_element_type=F32)
        place = jnp.full((1, 128), -1.0, F32)
        for k in range(keys):
            place = jnp.where(key == k, rank[k : k + 1] + float(k * WIDTH), place)
        place = jnp.broadcast_to(place, (8, 128)).T[:, 0:1].astype(jnp.int32)
        spots = lax.broadcasted_iota(jnp.int32, (128, width), 1)
        at_spot = jnp.where(place == spots, 1.0, 0.0).astype(BF16)
        fields = [slot.astype(F32), take.astype(F32), to.astype(F32), jnp.ones((1, 128), F32)]
        fields = jnp.concatenate(fields + [jnp.zeros((4, 128), F32)]).astype(BF16)
        found = jnp.dot(fields, at_spot, preferred_element_type=F32).astype(jnp.int32)
        entry = found[0:1] + found[1:2] * 2**8 + found[2:3] * 2**16
        entry = jnp.where(found[3:4] > 0, entry, pad * 2**16)
        total = jnp.sum(is_key.astype(F32), axis=1, keepdims=True).astype(jnp.int32)
        for k in range(keys):
            groups = (total[k : k + 1] + (UNROLL - 1)) // UNROLL
            entry = jnp.where(spots[0:1] == keys * WIDTH + k, groups, entry)
        return entry

    forward_tab[...] = table(1 - half, 2, ahead * 2 + cols % 2, pos, 32, TAB)
    key = jnp.where(half == 0, 0, jnp.where(ahead == 0, 2, 1))
    backward_tab[...] = table(key, 3, pos, ahead * 2 + cols % 2, 8, BACKWARD_TAB)


def hold(x, adj, x_held, tiles):
    x_held[...] = x[...]

    def copy(i, _):
        tiles[i] = adj[i]
        return 0

    lax.fori_loop(0, 128, copy, 0, unroll=8)


def each_tile(tab, key, keys, adj, product, acc):
    def body(g, _):
        parts = []
        for u in range(UNROLL):
            e = tab[0, key * WIDTH + g * UNROLL + u]
            parts.append((product(adj[e & 127], (e >> 8) & 63), e >> 16))
        for part, to in parts:
            acc[to] += part
        return 0

    lax.fori_loop(0, tab[0, keys * WIDTH + key], body, 0)


def load_blocks(refs, rows, to):
    for k, ref in enumerate(refs):
        for i in range(rows // B):
            to[k * (rows // B) + i] = ref[i * B : (i + 1) * B]


def forward_tiles(key, tab, x0, x1, x2, x3, adj, out, *scratch):
    acc, xs = scratch if key == 0 else (out, scratch[0])
    load_blocks([x0, x1, x2, x3], 256, xs)

    def clear(i, _):
        acc[i] = jnp.zeros((B, B), F32)
        return 0

    lax.fori_loop(0, 32, clear, 0)
    each_tile(tab, key, 2, adj, lambda t, i: jnp.dot(t, xs[i], preferred_element_type=F32), acc)
    if key == 0:

        def store(i, _):
            out[pl.ds(pl.multiple_of(i * B, B), B)] = acc[i].astype(BF16)
            return 0

        lax.fori_loop(0, 32, store, 0)


def core_sum(acc, got, m0, m1, m2, m3):
    for k, m in enumerate((m0, m1, m2, m3)):
        for i in range(8):
            rows = pl.ds((k * 8 + i) * B, B)
            total = acc[k * 8 + i] + got[rows].astype(F32)
            m[i * B : (i + 1) * B] = total.astype(m.dtype)


def first_sum(m0, r1, r2, r3, cot, total, msg):
    for i in range(0, 1024, 256):
        rows = pl.ds(i, 256)
        t = m0[rows] + (r1[rows].astype(F32) + r2[rows].astype(F32) + r3[rows].astype(F32))
        total[rows] = t
        msg[rows] = t.astype(BF16)
    msg[1024:1280] = cot[:, 0:B]
    msg[1280:1536] = cot[:, B : 2 * B]


def put_tail(msg, base, wg, bg):
    msg[pl.ds(base, 256)] = wg.astype(msg.dtype)
    if msg.dtype == F32:
        msg[pl.ds(base + 256, 16)] = jnp.concatenate([bg, jnp.zeros((14, B), F32)])
    else:
        high = bg.astype(BF16).astype(F32)
        low = bg - high
        block = jnp.concatenate([high, low, jnp.zeros((12, B), F32)])
        msg[pl.ds(base + 256, 16)] = block.astype(BF16)


def get_tail(msg, base):
    wg = msg[pl.ds(base, 256)].astype(F32)
    block = msg[pl.ds(base + 256, 16)].astype(F32)
    return wg, block[0:2] + block[2:4]


def local(s0, r1, r2, r3, weight, bias, cot, act, msg):
    w = weight[...]
    over_nodes = (((0,), (0,)), ((), ()))
    wg, bg = jnp.zeros((B, 256), F32), jnp.zeros((1, 256), F32)
    for k, r in enumerate((None, r3, r2, r1)):
        if k == 0:
            c = cot[...]
        else:
            c = jnp.concatenate([r[1024:1280], r[1280:1536]], axis=1)
        y = s0[pl.ds(k * 256, 256)]
        for d, r in ((1, r1), (2, r2), (3, r3)):
            y += r[pl.ds((k + d) % 4 * 256, 256)].astype(F32)
        y_high = y.astype(BF16)
        y_low = (y - y_high.astype(F32)).astype(BF16)
        summed = jnp.dot(y_high, w, preferred_element_type=F32) + jnp.dot(
            y_low, w, preferred_element_type=F32
        )
        pre = summed + bias[...]
        sig = jax.nn.sigmoid(pre)
        if k == 0:
            act[...] = (pre * sig).astype(BF16)
        slope = sig * (1.0 + pre * (1.0 - sig))
        grad = (c.astype(F32) * slope).astype(BF16)
        g = lax.dot_general(w, grad, (((1,), (1,)), ((), ())), preferred_element_type=F32)
        g = g.astype(BF16)
        msg[pl.ds(k * 256, B)] = g[:, 0:B]
        msg[pl.ds(k * 256 + B, B)] = g[:, B : 2 * B]
        wg += lax.dot_general(y_high, grad, over_nodes, preferred_element_type=F32)
        wg += lax.dot_general(y_low, grad, over_nodes, preferred_element_type=F32)
        bg += jnp.sum(grad.astype(F32), axis=0, keepdims=True)
    put_tail(
        msg,
        1024,
        jnp.concatenate([wg[:, 0:B], wg[:, B : 2 * B]]),
        jnp.concatenate([bg[:, 0:B], bg[:, B : 2 * B]]),
    )


def sum_tails(pieces):
    wg, bg = get_tail(pieces[0], 1024)
    for piece in pieces[1:]:
        wg_r, bg_r = get_tail(piece, 1024)
        wg += wg_r
        bg += bg_r
    return wg, bg


def backward_tiles(key, tab, adj, *refs):
    def product(t, i):
        return jnp.dot(gs[i], t, preferred_element_type=F32)

    if key == 0:
        pieces, (acc, tail, gs) = refs[:4], refs[4:]
        load_blocks(pieces, 1024, gs)
        acc[...] = jnp.zeros((9, B, B), F32)
        each_tile(tab, 0, 3, adj, product, acc)
        put_tail(tail, 0, *sum_tails(pieces))
        return
    if key == 1:
        pieces, (acc_in, tail_in, m1, m2, m3, gs, tail, acc) = refs[:4], refs[4:]
        outs = (m1, m2, m3)
        load_blocks(pieces, 1024, gs)
        wg, bg = sum_tails(pieces)
        put_tail(tail, 0, tail_in[0:256] + wg, tail_in[256:258] + bg)
    else:
        gs, acc_in, tail, m0, acc = refs
        outs = (m0,)
    first = 2 if key == 1 else 0
    last = first + 2 * len(outs)
    acc[first:last] = acc_in[first:last]
    each_tile(tab, key, 3, adj, product, acc)
    for k, m in enumerate(outs):
        m[0:B] = acc[first + 2 * k].astype(m.dtype)
        m[B : 2 * B] = acc[first + 2 * k + 1].astype(m.dtype)
        put_tail(m, 256, tail[0:256], tail[256:258])


def last_sum(m0, r1, r2, r3, feat, wgrad, bgrad):
    for k in range(2):
        rows = pl.ds(k * B, B)
        total = m0[rows] + (r1[rows].astype(F32) + r2[rows].astype(F32) + r3[rows].astype(F32))
        feat[rows] = total.T.astype(BF16)
    wg, block = m0[pl.ds(256, 256)], m0[pl.ds(512, 16)]
    bg = block[0:2]
    for r in (r1, r2, r3):
        wg_r, bg_r = get_tail(r, 256)
        wg += wg_r
        bg += bg_r
    wgrad[:, 0:B] = wg[0:B]
    wgrad[:, B : 2 * B] = wg[B : 2 * B]
    bgrad[:, 0:B] = bg[0:1]
    bgrad[:, B : 2 * B] = bg[1:2]


def on_device(
    features, weight, bias_vector, adjacency, tile_rows, tile_cols, tile_count, cotangent
):
    adj = adjacency[0, 0]
    x2, x1, x3 = permute([features] * 3, "row", [row_shift(d) for d in ORDER])
    live = call(live_slots, sds(1, 128, jnp.int32), [SMEM], nbytes=LEAD)(tile_count)
    forward_tab, backward_tab = call(
        sort_tiles,
        (sds(1, TAB, jnp.int32), sds(1, BACKWARD_TAB, jnp.int32)),
        [VMEM] * 3,
    )(tile_rows[0], tile_cols[0], live)
    x0, tiles = call(
        hold, (sds(256), jax.ShapeDtypeStruct((128, B, B), BF16)), [VMEM, VMEM]
    )(features, adj)
    xs = (x0, x3, x2, x1)
    half = jax.ShapeDtypeStruct((33, B, B), F32)
    other = call(
        functools.partial(forward_tiles, 0),
        sds(4096),
        [SMEM] + [VMEM] * 5,
        [pltpu.VMEM((33, B, B), F32), pltpu.VMEM((8, B, B), BF16)],
        tiles=64,
    )(forward_tab, *xs, tiles)
    got = lax.ppermute(other, "col", core_swap())
    acc = call(
        functools.partial(forward_tiles, 1),
        half,
        [SMEM] + [VMEM] * 5,
        [pltpu.VMEM((8, B, B), BF16)],
    )(forward_tab, *xs, tiles)
    ms = call(core_sum, (sds(1024, dtype=F32),) + (sds(1024),) * 3, [VMEM] * 2)(acc, got)
    r2, r1, r3 = permute([ms[d] for d in ORDER], "col", [col_shift(True, d) for d in ORDER])
    total, msg = call(first_sum, (sds(1024, dtype=F32), sds(1536)), [VMEM] * 5)(
        ms[0], r1, r2, r3, cotangent
    )
    r2, r1, r3 = permute([msg] * 3, "col", [col_shift(False, d) for d in ORDER])
    act, msg = call(local, (sds(256, 256), sds(1024 + TAIL)), [VMEM] * 7)(
        total, r1, r2, r3, weight, bias_vector.reshape(1, 256), cotangent
    )
    r2, r1, r3 = permute([msg] * 3, "col", [col_shift(True, d) for d in ORDER])
    mine = (msg, r3, r2, r1)
    theirs = [lax.ppermute(m, "col", core_swap()) for m in mine]
    out, tail = sds(256 + TAIL), sds(TAIL, dtype=F32)
    sums, blocks = (jax.ShapeDtypeStruct(s, t) for s, t in (((9, B, B), F32), ((32, B, B), BF16)))
    sums, tail = call(
        functools.partial(backward_tiles, 0),
        (sums, tail),
        [SMEM] + [VMEM] * 5,
        [pltpu.VMEM((32, B, B), BF16)],
        tiles=64,
    )(backward_tab, adj, *mine)
    *ms, blocks, tail = call(
        functools.partial(backward_tiles, 1),
        (out, out, out, blocks, sds(TAIL, dtype=F32)),
        [SMEM] + [VMEM] * 7,
        [pltpu.VMEM((9, B, B), F32)],
        tiles=48,
    )(backward_tab, adj, *theirs, sums, tail)
    m = call(
        functools.partial(backward_tiles, 2),
        sds(256 + TAIL, dtype=F32),
        [SMEM] + [VMEM] * 4,
        [pltpu.VMEM((9, B, B), F32)],
    )(backward_tab, adj, blocks, sums, tail)
    ms = [ms[d - 1] for d in ORDER]
    rs = [lax.ppermute(a, "row", row_shift(d)) for a, d in zip(ms, ORDER)]
    feat, wgrad, bgrad = call(
        last_sum, (sds(256, 128), sds(128, 256, F32), sds(1, 256, F32)), [VMEM] * 4
    )(m, *rs)
    return (act, feat, wgrad, bgrad.reshape(256))


def solution(mesh):
    placed = (
        P(("row", "col"), None),
        P(),
        P(),
        P("row", "col", None, None, None),
        P("row", "col", None),
        P("row", "col", None),
        P("row", "col"),
        P(("row", "col"), None),
    )
    return jax.shard_map(
        on_device,
        mesh=mesh,
        in_specs=placed,
        out_specs=(P(("row", "col"), None), P(("row", "col"), None), P(), P()),
        check_vma=False,
    )
```

```python
import functools

import jax
import jax.numpy as jnp
from jax import lax
from jax.experimental import pallas as pl
from jax.experimental.pallas import tpu as pltpu
from jax.sharding import PartitionSpec as P

F32 = jnp.float32
BF16 = jnp.bfloat16
B = 128
VMEM = pl.BlockSpec(memory_space=pltpu.VMEM)
SMEM = pl.BlockSpec(memory_space=pltpu.SMEM)
ANY = pl.BlockSpec(memory_space=pl.ANY)
TAIL = 272
UNROLL = 16
WIDTH = 144
TAB = 384
BACKWARD_TAB = 640


def at(y, z, core):
    return (y * 4 + z) * 2 + core


def col_shift(first, d):
    pairs = []
    for y in range(4):
        for z in range(4):
            for core in range(2):
                along_z = (core == 0) == first
                to = at(y, (z + d) % 4, core) if along_z else at((y + d) % 4, z, core)
                pairs.append((at(y, z, core), to))
    return pairs


def core_swap():
    return [(c, c ^ 1) for c in range(32)]


def row_shift(d):
    return [(r, (r + d) % 4) for r in range(4)]


def call(kernel, outs, ins, scratch=(), tiles=0, nbytes=0, aliases=None, limit=24):
    return pl.pallas_call(
        kernel,
        out_shape=outs,
        in_specs=ins,
        out_specs=jax.tree.map(lambda _: VMEM, outs),
        scratch_shapes=list(scratch),
        input_output_aliases=aliases or {},
        compiler_params=pltpu.CompilerParams(vmem_limit_bytes=limit * 2**20),
        cost_estimate=pl.CostEstimate(
            flops=2 * tiles * B**3, bytes_accessed=nbytes + tiles * 2**16, transcendentals=0
        ),
    )


def sds(rows, cols=B, dtype=BF16):
    return jax.ShapeDtypeStruct((rows, cols), dtype)


def permute(arrays, axis, pairs):
    arrays = lax.optimization_barrier(tuple(arrays))
    return lax.optimization_barrier([lax.ppermute(a, axis, p) for a, p in zip(arrays, pairs)])


ORDER = (1, 3, 2)


def sort_tiles(rows, cols, count, forward_tab, backward_tab):
    r, c = lax.axis_index("row"), lax.axis_index("col")
    core, z, y = c % 2, (c // 2) % 4, c // 8
    rows, cols = rows[...], cols[...]
    owner, sub = rows // 2, rows % 2
    core_to, z_to, y_to = owner % 2, (owner // 2) % 4, owner // 8
    dz, dy = (z_to - z + 4) % 4, (y_to - y + 4) % 4
    first = jnp.where(core_to == 0, dz, dy)
    second = jnp.where(core_to == 0, dy, dz)
    pos = (first * 4 + second) * 2 + sub
    half = (core_to != core).astype(jnp.int32)
    ahead = (cols // 2 - r + 4) % 4
    slot = lax.broadcasted_iota(jnp.int32, (1, 128), 1)

    def table(key, keys, take, to, pad, width):
        key = jnp.where(slot < count[0, 0], key, keys)
        is_key = [jnp.where(key == k, 1.0, 0.0) for k in range(keys)]
        is_key = jnp.concatenate(is_key + [jnp.zeros((8 - keys, 128), F32)]).astype(BF16)
        low = lax.broadcasted_iota(jnp.int32, (128, 128), 0)
        high = lax.broadcasted_iota(jnp.int32, (128, 128), 1)
        before = jnp.where(low < high, 1.0, 0.0).astype(BF16)
        rank = jnp.dot(is_key, before, preferred_element_type=F32)
        place = jnp.full((1, 128), -1.0, F32)
        for k in range(keys):
            place = jnp.where(key == k, rank[k : k + 1] + float(k * WIDTH), place)
        place = jnp.broadcast_to(place, (8, 128)).T[:, 0:1].astype(jnp.int32)
        spots = lax.broadcasted_iota(jnp.int32, (128, width), 1)
        at_spot = jnp.where(place == spots, 1.0, 0.0).astype(BF16)
        fields = [slot.astype(F32), take.astype(F32), to.astype(F32), jnp.ones((1, 128), F32)]
        fields = jnp.concatenate(fields + [jnp.zeros((4, 128), F32)]).astype(BF16)
        found = jnp.dot(fields, at_spot, preferred_element_type=F32).astype(jnp.int32)
        entry = found[0:1] + found[1:2] * 2**8 + found[2:3] * 2**16
        entry = jnp.where(found[3:4] > 0, entry, pad * 2**16)
        total = jnp.sum(is_key.astype(F32), axis=1, keepdims=True).astype(jnp.int32)
        for k in range(keys):
            groups = (total[k : k + 1] + (UNROLL - 1)) // UNROLL
            entry = jnp.where(spots[0:1] == keys * WIDTH + k, groups, entry)
        return entry

    forward_tab[...] = table(1 - half, 2, ahead * 2 + cols % 2, pos, 32, TAB)
    late = (first == 1).astype(jnp.int32)
    key = jnp.where(half + late < 2, half + late, jnp.where(ahead == 0, 3, 2))
    take = half * 32 + pos
    backward_tab[...] = table(key, 4, take, ahead * 2 + cols % 2, 8, BACKWARD_TAB)


def hold(adj, tiles, acc0, acc1, sem):
    n = sem.shape[0]
    parts = [pl.ds(k * (128 // n), 128 // n) for k in range(n)]
    copies = [
        pltpu.make_async_copy(adj.at[part], tiles.at[part], sem.at[k])
        for k, part in enumerate(parts)
    ]
    for copy in copies:
        copy.start()

    def block(i, _):
        acc0[i] = jnp.zeros((B, B), F32)
        acc1[i] = jnp.zeros((B, B), F32)
        return 0

    lax.fori_loop(0, 32, block, 0, unroll=4)
    for copy in copies:
        copy.wait()


def each_tile(tab, key, keys, adj, product, acc):
    def body(g, _):
        parts = []
        for u in range(UNROLL):
            e = tab[0, key * WIDTH + g * UNROLL + u]
            parts.append((product(adj[e & 127], (e >> 8) & 63), e >> 16))
        for part, to in parts:
            acc[to] += part
        return 0

    lax.fori_loop(0, tab[0, keys * WIDTH + key], body, 0)


def load_blocks(refs, rows, to):
    for k, ref in enumerate(refs):
        for i in range(rows // B):
            to[k * (rows // B) + i] = ref[i * B : (i + 1) * B]


def forward_tiles(key, tab, x0, x1, x2, x3, adj, _, acc, *refs):
    *out, xs, sem = refs
    copies = [
        pltpu.make_async_copy(x0.at[pl.ds(k * B, B)], xs.at[k], sem.at[k]) for k in range(2)
    ]
    for copy in copies:
        copy.start()
    load_blocks([x1, x2, x3], 256, xs.at[pl.ds(2, 6)])
    for copy in copies:
        copy.wait()
    each_tile(tab, key, 2, adj, lambda t, i: jnp.dot(t, xs[i], preferred_element_type=F32), acc)
    if key == 0:

        def store(i, _):
            out[0][pl.ds(pl.multiple_of(i * B, B), B)] = acc[i].astype(BF16)
            return 0

        lax.fori_loop(0, 32, store, 0, unroll=4)


def core_sum(acc, got, m0, m1, m2, m3):
    for k, m in enumerate((m0, m1, m2, m3)):
        for i in range(8):
            rows = pl.ds((k * 8 + i) * B, B)
            total = acc[k * 8 + i] + got[rows].astype(F32)
            m[i * B : (i + 1) * B] = total.astype(m.dtype)


def first_sum(m0, r1, r2, r3, cot, total, msg):
    for i in range(0, 1024, 256):
        rows = pl.ds(i, 256)
        t = m0[rows] + (r1[rows].astype(F32) + r2[rows].astype(F32) + r3[rows].astype(F32))
        total[rows] = t
        msg[rows] = t.astype(BF16)
    msg[1024:1280] = cot[:, 0:B]
    msg[1280:1536] = cot[:, B : 2 * B]


def put_tail(msg, base, wg, bg):
    msg[pl.ds(base, 256)] = wg.astype(msg.dtype)
    if msg.dtype == F32:
        msg[pl.ds(base + 256, 16)] = jnp.concatenate([bg, jnp.zeros((14, B), F32)])
    else:
        high = bg.astype(BF16).astype(F32)
        low = bg - high
        block = jnp.concatenate([high, low, jnp.zeros((12, B), F32)])
        msg[pl.ds(base + 256, 16)] = block.astype(BF16)


def get_tail(msg, base):
    wg = msg[pl.ds(base, 256)].astype(F32)
    block = msg[pl.ds(base + 256, 16)].astype(F32)
    return wg, block[0:2] + block[2:4]


def local(s0, r1, r2, r3, weight, bias, cot, act, msg):
    w = weight[...]
    over_nodes = (((0,), (0,)), ((), ()))
    wg, bg = jnp.zeros((B, 256), F32), jnp.zeros((1, 256), F32)
    for k, r in enumerate((None, r3, r2, r1)):
        if k == 0:
            c = cot[...]
        else:
            c = jnp.concatenate([r[1024:1280], r[1280:1536]], axis=1)
        y = s0[pl.ds(k * 256, 256)]
        for d, r in ((1, r1), (2, r2), (3, r3)):
            y += r[pl.ds((k + d) % 4 * 256, 256)].astype(F32)
        y_high = y.astype(BF16)
        y_low = (y - y_high.astype(F32)).astype(BF16)
        summed = jnp.dot(y_high, w, preferred_element_type=F32) + jnp.dot(
            y_low, w, preferred_element_type=F32
        )
        pre = summed + bias[...]
        sig = jax.nn.sigmoid(pre)
        if k == 0:
            act[...] = (pre * sig).astype(BF16)
        slope = sig * (1.0 + pre * (1.0 - sig))
        grad = (c.astype(F32) * slope).astype(BF16)
        g = lax.dot_general(w, grad, (((1,), (1,)), ((), ())), preferred_element_type=F32)
        g = g.astype(BF16)
        msg[pl.ds(k * 256, B)] = g[:, 0:B]
        msg[pl.ds(k * 256 + B, B)] = g[:, B : 2 * B]
        wg += lax.dot_general(y_high, grad, over_nodes, preferred_element_type=F32)
        wg += lax.dot_general(y_low, grad, over_nodes, preferred_element_type=F32)
        bg += jnp.sum(grad.astype(F32), axis=0, keepdims=True)
    put_tail(
        msg,
        1024,
        jnp.concatenate([wg[:, 0:B], wg[:, B : 2 * B]]),
        jnp.concatenate([bg[:, 0:B], bg[:, B : 2 * B]]),
    )


def sum_tails(pieces):
    wg, bg = get_tail(pieces[0], 1024)
    for piece in pieces[1:]:
        wg_r, bg_r = get_tail(piece, 1024)
        wg += wg_r
        bg += bg_r
    return wg, bg


def backward_tiles(key, places, tab, adj, *refs):
    def product(t, i):
        return jnp.dot(gs[i], t, preferred_element_type=F32)

    pieces, refs, gs = refs[: len(places)], refs[len(places) : -1], refs[-1]
    for place, piece in zip(places, pieces):
        load_blocks([piece], 1024, gs.at[pl.ds(place * 8, 8)])
    if key < 2:
        if key == 0:
            acc, tail = refs
            acc[...] = jnp.zeros((9, B, B), F32)
        else:
            _, tail_in, acc, tail = refs
        each_tile(tab, key, 4, adj, product, acc)
        wg, bg = sum_tails(pieces)
        if key == 1:
            wg, bg = wg + tail_in[0:256], bg + tail_in[256:258]
        put_tail(tail, 0, wg, bg)
        return
    acc_in, tail_in, *outs, acc = refs
    first = 2 if key == 2 else 0
    last = first + 2 * len(outs)
    acc[first:last] = acc_in[first:last]
    each_tile(tab, key, 4, adj, product, acc)
    wg, bg = sum_tails(pieces)
    wg, bg = wg + tail_in[0:256], bg + tail_in[256:258]
    for k, m in enumerate(outs):
        m[0:B] = acc[first + 2 * k].astype(m.dtype)
        m[B : 2 * B] = acc[first + 2 * k + 1].astype(m.dtype)
        put_tail(m, 256, wg, bg)


def last_sum(m0, r1, r2, r3, feat, wgrad, bgrad):
    for k in range(2):
        rows = pl.ds(k * B, B)
        total = m0[rows] + (r1[rows].astype(F32) + r2[rows].astype(F32) + r3[rows].astype(F32))
        feat[rows] = total.T.astype(BF16)
    wg, block = m0[pl.ds(256, 256)], m0[pl.ds(512, 16)]
    bg = block[0:2]
    for r in (r1, r2, r3):
        wg_r, bg_r = get_tail(r, 256)
        wg += wg_r
        bg += bg_r
    wgrad[:, 0:B] = wg[0:B]
    wgrad[:, B : 2 * B] = wg[B : 2 * B]
    bgrad[:, 0:B] = bg[0:1]
    bgrad[:, B : 2 * B] = bg[1:2]


def on_device(
    features, weight, bias_vector, adjacency, tile_rows, tile_cols, tile_count, cotangent
):
    adj = adjacency[0, 0]
    x1, x3, x2 = permute([features] * 3, "row", [row_shift(d) for d in ORDER])
    forward_tab, backward_tab = call(
        sort_tiles,
        (sds(1, TAB, jnp.int32), sds(1, BACKWARD_TAB, jnp.int32)),
        [VMEM, VMEM, SMEM],
    )(tile_rows[0], tile_cols[0], tile_count)
    half = jax.ShapeDtypeStruct((33, B, B), F32)
    tiles, acc0, acc1 = call(
        hold,
        (jax.ShapeDtypeStruct((128, B, B), BF16), half, half),
        [ANY],
        [pltpu.SemaphoreType.DMA((8,))],
        limit=43,
    )(adj)
    xs = (features, x3, x2, x1)
    scratch = [pltpu.VMEM((8, B, B), BF16), pltpu.SemaphoreType.DMA((2,))]
    _, other = call(
        functools.partial(forward_tiles, 0),
        (half, sds(4096)),
        [SMEM, ANY] + [VMEM] * 5,
        scratch,
        tiles=64,
        aliases={6: 0},
    )(forward_tab, *xs, tiles, acc0)
    got = lax.ppermute(other, "col", core_swap())
    acc = call(
        functools.partial(forward_tiles, 1),
        half,
        [SMEM, ANY] + [VMEM] * 5,
        scratch,
        aliases={6: 0},
    )(forward_tab, *xs, tiles, acc1)
    ms = call(core_sum, (sds(1024, dtype=F32),) + (sds(1024),) * 3, [VMEM] * 2)(acc, got)
    r1, r3, r2 = permute([ms[d] for d in ORDER], "col", [col_shift(True, d) for d in ORDER])
    total, msg = call(first_sum, (sds(1024, dtype=F32), sds(1536)), [VMEM] * 5)(
        ms[0], r1, r2, r3, cotangent
    )
    r1, r3, r2 = permute([msg] * 3, "col", [col_shift(False, d) for d in ORDER])
    act, msg = call(local, (sds(256, 256), sds(1024 + TAIL)), [VMEM] * 7)(
        total, r1, r2, r3, weight, bias_vector.reshape(1, 256), cotangent
    )
    r1, r3, r2 = permute([msg] * 3, "col", [col_shift(True, d) for d in ORDER])
    mine = (msg, r3, r2, r1)
    theirs = [lax.ppermute(m, "col", core_swap()) for m in mine]
    out, tail = sds(256 + TAIL), sds(TAIL, dtype=F32)
    sums = jax.ShapeDtypeStruct((9, B, B), F32)
    blocks, acc = pltpu.VMEM((64, B, B), BF16), pltpu.VMEM((9, B, B), F32)

    def backward(key, places, outs, scratch, tiles, aliases, *extra):
        pieces = [(mine + tuple(theirs))[p] for p in places]
        return call(
            functools.partial(backward_tiles, key, places),
            outs,
            [SMEM] + [VMEM] * (1 + len(places) + len(extra)),
            scratch,
            tiles=tiles,
            aliases=aliases,
        )(backward_tab, adj, *pieces, *extra)

    state = backward(0, (0, 2, 3), (sums, tail), [blocks], 48, None)
    state = backward(1, (1, 4, 6, 7), (sums, tail), [blocks], 64, {6: 0}, *state)
    ms = backward(2, (5,), (out,) * 3, [acc, blocks], 16, None, *state)
    (m,) = backward(3, (5,), (sds(256 + TAIL, dtype=F32),), [acc, blocks], 0, None, *state)
    ms = [ms[d - 1] for d in ORDER]
    rs = [lax.ppermute(a, "row", row_shift(d)) for a, d in zip(ms, ORDER)]
    feat, wgrad, bgrad = call(
        last_sum, (sds(256, 128), sds(128, 256, F32), sds(1, 256, F32)), [VMEM] * 4
    )(m, *rs)
    return (act, feat, wgrad, bgrad.reshape(256))


def solution(mesh):
    placed = (
        P(("row", "col"), None),
        P(),
        P(),
        P("row", "col", None, None, None),
        P("row", "col", None),
        P("row", "col", None),
        P("row", "col"),
        P(("row", "col"), None),
    )
    return jax.shard_map(
        on_device,
        mesh=mesh,
        in_specs=placed,
        out_specs=(P(("row", "col"), None), P(("row", "col"), None), P(), P()),
        check_vma=False,
    )
```

```python
import functools

import jax
import jax.numpy as jnp
from jax import lax
from jax.experimental import pallas as pl
from jax.experimental.pallas import tpu as pltpu
from jax.sharding import PartitionSpec as P

F32 = jnp.float32
BF16 = jnp.bfloat16
B = 128
VMEM = pl.BlockSpec(memory_space=pltpu.VMEM)
SMEM = pl.BlockSpec(memory_space=pltpu.SMEM)
ANY = pl.BlockSpec(memory_space=pl.ANY)
TAIL = 272
UNROLL = 16
WIDTH = 144
TAB = 384
BACKWARD_TAB = 640


def at(y, z, core):
    return (y * 4 + z) * 2 + core


def ring_of(y, z, core):
    return (core + y + z) % 2


def col_shift(first, d):
    pairs = []
    for y in range(4):
        for z in range(4):
            for core in range(2):
                ring = ring_of(y, z, core)
                along_z = (ring == 0) == first
                to_y, to_z = (y, (z + d) % 4) if along_z else ((y + d) % 4, z)
                pairs.append((at(y, z, core), at(to_y, to_z, ring_of(to_y, to_z, ring))))
    return pairs


def core_swap():
    return [(c, c ^ 1) for c in range(32)]


def row_shift(d):
    return [(r, (r + d) % 4) for r in range(4)]


def call(kernel, outs, ins, scratch=(), tiles=0, nbytes=0, aliases=None, limit=24):
    return pl.pallas_call(
        kernel,
        out_shape=outs,
        in_specs=ins,
        out_specs=jax.tree.map(lambda _: VMEM, outs),
        scratch_shapes=list(scratch),
        input_output_aliases=aliases or {},
        compiler_params=pltpu.CompilerParams(vmem_limit_bytes=limit * 2**20),
        cost_estimate=pl.CostEstimate(
            flops=2 * tiles * B**3, bytes_accessed=nbytes + tiles * 2**16, transcendentals=0
        ),
    )


def sds(rows, cols=B, dtype=BF16):
    return jax.ShapeDtypeStruct((rows, cols), dtype)


def permute(arrays, axis, pairs):
    arrays = lax.optimization_barrier(tuple(arrays))
    return lax.optimization_barrier([lax.ppermute(a, axis, p) for a, p in zip(arrays, pairs)])


ORDER = (1, 3, 2)


def sort_tiles(rows, cols, count, forward_tab, backward_tab):
    r, c = lax.axis_index("row"), lax.axis_index("col")
    core, z, y = c % 2, (c // 2) % 4, c // 8
    rows, cols = rows[...], cols[...]
    owner, sub = rows // 2, rows % 2
    core_to, z_to, y_to = owner % 2, (owner // 2) % 4, owner // 8
    dz, dy = (z_to - z + 4) % 4, (y_to - y + 4) % 4
    ring_to = ring_of(y_to, z_to, core_to)
    first = jnp.where(ring_to == 0, dz, dy)
    second = jnp.where(ring_to == 0, dy, dz)
    pos = (first * 4 + second) * 2 + sub
    half = (ring_to != ring_of(y, z, core)).astype(jnp.int32)
    ahead = (cols // 2 - r + 4) % 4
    slot = lax.broadcasted_iota(jnp.int32, (1, 128), 1)

    def table(key, keys, take, to, pad, width):
        key = jnp.where(slot < count[0, 0], key, keys)
        is_key = [jnp.where(key == k, 1.0, 0.0) for k in range(keys)]
        is_key = jnp.concatenate(is_key + [jnp.zeros((8 - keys, 128), F32)]).astype(BF16)
        low = lax.broadcasted_iota(jnp.int32, (128, 128), 0)
        high = lax.broadcasted_iota(jnp.int32, (128, 128), 1)
        before = jnp.where(low < high, 1.0, 0.0).astype(BF16)
        rank = jnp.dot(is_key, before, preferred_element_type=F32)
        place = jnp.full((1, 128), -1.0, F32)
        for k in range(keys):
            place = jnp.where(key == k, rank[k : k + 1] + float(k * WIDTH), place)
        place = jnp.broadcast_to(place, (8, 128)).T[:, 0:1].astype(jnp.int32)
        spots = lax.broadcasted_iota(jnp.int32, (128, width), 1)
        at_spot = jnp.where(place == spots, 1.0, 0.0).astype(BF16)
        fields = [slot.astype(F32), take.astype(F32), to.astype(F32), jnp.ones((1, 128), F32)]
        fields = jnp.concatenate(fields + [jnp.zeros((4, 128), F32)]).astype(BF16)
        found = jnp.dot(fields, at_spot, preferred_element_type=F32).astype(jnp.int32)
        entry = found[0:1] + found[1:2] * 2**8 + found[2:3] * 2**16
        entry = jnp.where(found[3:4] > 0, entry, pad * 2**16)
        total = jnp.sum(is_key.astype(F32), axis=1, keepdims=True).astype(jnp.int32)
        for k in range(keys):
            groups = (total[k : k + 1] + (UNROLL - 1)) // UNROLL
            entry = jnp.where(spots[0:1] == keys * WIDTH + k, groups, entry)
        return entry

    forward_tab[...] = table(1 - half, 2, ahead * 2 + cols % 2, pos, 32, TAB)
    late = (first == 1).astype(jnp.int32)
    key = jnp.where(half + late < 2, half + late, jnp.where(ahead == 0, 3, 2))
    take = half * 32 + pos
    backward_tab[...] = table(key, 4, take, ahead * 2 + cols % 2, 8, BACKWARD_TAB)


def hold(adj, tiles, acc0, acc1, sem):
    n = sem.shape[0]
    parts = [pl.ds(k * (128 // n), 128 // n) for k in range(n)]
    copies = [
        pltpu.make_async_copy(adj.at[part], tiles.at[part], sem.at[k])
        for k, part in enumerate(parts)
    ]
    for copy in copies:
        copy.start()

    def block(i, _):
        acc0[i] = jnp.zeros((B, B), F32)
        acc1[i] = jnp.zeros((B, B), F32)
        return 0

    lax.fori_loop(0, 32, block, 0, unroll=4)
    for copy in copies:
        copy.wait()


def each_tile(tab, key, keys, adj, product, acc):
    def body(g, _):
        parts = []
        for u in range(UNROLL):
            e = tab[0, key * WIDTH + g * UNROLL + u]
            parts.append((product(adj[e & 127], (e >> 8) & 63), e >> 16))
        for part, to in parts:
            acc[to] += part
        return 0

    lax.fori_loop(0, tab[0, keys * WIDTH + key], body, 0)


def load_blocks(refs, rows, to):
    for k, ref in enumerate(refs):
        for i in range(rows // B):
            to[k * (rows // B) + i] = ref[i * B : (i + 1) * B]


def forward_tiles(key, tab, x0, x1, x2, x3, adj, _, acc, *refs):
    *out, xs, sem = refs
    copies = [
        pltpu.make_async_copy(x0.at[pl.ds(k * B, B)], xs.at[k], sem.at[k]) for k in range(2)
    ]
    for copy in copies:
        copy.start()
    load_blocks([x1, x2, x3], 256, xs.at[pl.ds(2, 6)])
    for copy in copies:
        copy.wait()
    each_tile(tab, key, 2, adj, lambda t, i: jnp.dot(t, xs[i], preferred_element_type=F32), acc)
    if key == 0:

        def store(i, _):
            out[0][pl.ds(pl.multiple_of(i * B, B), B)] = acc[i].astype(BF16)
            return 0

        lax.fori_loop(0, 32, store, 0, unroll=4)


def core_sum(acc, got, m0, m1, m2, m3):
    for k, m in enumerate((m0, m1, m2, m3)):
        for i in range(8):
            rows = pl.ds((k * 8 + i) * B, B)
            total = acc[k * 8 + i] + got[rows].astype(F32)
            m[i * B : (i + 1) * B] = total.astype(m.dtype)


def first_sum(m0, r1, r2, r3, cot, total, msg):
    for i in range(0, 1024, 256):
        rows = pl.ds(i, 256)
        t = m0[rows] + (r1[rows].astype(F32) + r2[rows].astype(F32) + r3[rows].astype(F32))
        total[rows] = t
        msg[rows] = t.astype(BF16)
    msg[1024:1280] = cot[:, 0:B]
    msg[1280:1536] = cot[:, B : 2 * B]


def put_tail(msg, base, wg, bg):
    msg[pl.ds(base, 256)] = wg.astype(msg.dtype)
    if msg.dtype == F32:
        msg[pl.ds(base + 256, 16)] = jnp.concatenate([bg, jnp.zeros((14, B), F32)])
    else:
        high = bg.astype(BF16).astype(F32)
        low = bg - high
        block = jnp.concatenate([high, low, jnp.zeros((12, B), F32)])
        msg[pl.ds(base + 256, 16)] = block.astype(BF16)


def get_tail(msg, base):
    wg = msg[pl.ds(base, 256)].astype(F32)
    block = msg[pl.ds(base + 256, 16)].astype(F32)
    return wg, block[0:2] + block[2:4]


def local(s0, r1, r2, r3, weight, bias, cot, act, msg):
    w = weight[...]
    over_nodes = (((0,), (0,)), ((), ()))
    wg, bg = jnp.zeros((B, 256), F32), jnp.zeros((1, 256), F32)
    for k, r in enumerate((None, r3, r2, r1)):
        if k == 0:
            c = cot[...]
        else:
            c = jnp.concatenate([r[1024:1280], r[1280:1536]], axis=1)
        y = s0[pl.ds(k * 256, 256)]
        for d, r in ((1, r1), (2, r2), (3, r3)):
            y += r[pl.ds((k + d) % 4 * 256, 256)].astype(F32)
        y_high = y.astype(BF16)
        y_low = (y - y_high.astype(F32)).astype(BF16)
        summed = jnp.dot(y_high, w, preferred_element_type=F32) + jnp.dot(
            y_low, w, preferred_element_type=F32
        )
        pre = summed + bias[...]
        sig = jax.nn.sigmoid(pre)
        if k == 0:
            act[...] = (pre * sig).astype(BF16)
        slope = sig * (1.0 + pre * (1.0 - sig))
        grad = (c.astype(F32) * slope).astype(BF16)
        g = lax.dot_general(w, grad, (((1,), (1,)), ((), ())), preferred_element_type=F32)
        g = g.astype(BF16)
        msg[pl.ds(k * 256, B)] = g[:, 0:B]
        msg[pl.ds(k * 256 + B, B)] = g[:, B : 2 * B]
        wg += lax.dot_general(y_high, grad, over_nodes, preferred_element_type=F32)
        wg += lax.dot_general(y_low, grad, over_nodes, preferred_element_type=F32)
        bg += jnp.sum(grad.astype(F32), axis=0, keepdims=True)
    put_tail(
        msg,
        1024,
        jnp.concatenate([wg[:, 0:B], wg[:, B : 2 * B]]),
        jnp.concatenate([bg[:, 0:B], bg[:, B : 2 * B]]),
    )


def sum_tails(pieces):
    wg, bg = get_tail(pieces[0], 1024)
    for piece in pieces[1:]:
        wg_r, bg_r = get_tail(piece, 1024)
        wg += wg_r
        bg += bg_r
    return wg, bg


def backward_tiles(key, places, tab, adj, *refs):
    def product(t, i):
        return jnp.dot(gs[i], t, preferred_element_type=F32)

    pieces, refs, gs = refs[: len(places)], refs[len(places) : -1], refs[-1]
    for place, piece in zip(places, pieces):
        load_blocks([piece], 1024, gs.at[pl.ds(place * 8, 8)])
    if key < 2:
        if key == 0:
            acc, tail = refs
            acc[...] = jnp.zeros((9, B, B), F32)
        else:
            _, tail_in, acc, tail = refs
        each_tile(tab, key, 4, adj, product, acc)
        wg, bg = sum_tails(pieces)
        if key == 1:
            wg, bg = wg + tail_in[0:256], bg + tail_in[256:258]
        put_tail(tail, 0, wg, bg)
        return
    acc_in, tail_in, *outs, acc = refs
    first = 2 if key == 2 else 0
    last = first + 2 * len(outs)
    acc[first:last] = acc_in[first:last]
    each_tile(tab, key, 4, adj, product, acc)
    wg, bg = sum_tails(pieces)
    wg, bg = wg + tail_in[0:256], bg + tail_in[256:258]
    for k, m in enumerate(outs):
        m[0:B] = acc[first + 2 * k].astype(m.dtype)
        m[B : 2 * B] = acc[first + 2 * k + 1].astype(m.dtype)
        put_tail(m, 256, wg, bg)


def last_sum(m0, r1, r2, r3, feat, wgrad, bgrad):
    for k in range(2):
        rows = pl.ds(k * B, B)
        total = m0[rows] + (r1[rows].astype(F32) + r2[rows].astype(F32) + r3[rows].astype(F32))
        feat[rows] = total.T.astype(BF16)
    wg, block = m0[pl.ds(256, 256)], m0[pl.ds(512, 16)]
    bg = block[0:2]
    for r in (r1, r2, r3):
        wg_r, bg_r = get_tail(r, 256)
        wg += wg_r
        bg += bg_r
    wgrad[:, 0:B] = wg[0:B]
    wgrad[:, B : 2 * B] = wg[B : 2 * B]
    bgrad[:, 0:B] = bg[0:1]
    bgrad[:, B : 2 * B] = bg[1:2]


def on_device(
    features, weight, bias_vector, adjacency, tile_rows, tile_cols, tile_count, cotangent
):
    adj = adjacency[0, 0]
    x1, x3, x2 = permute([features] * 3, "row", [row_shift(d) for d in ORDER])
    forward_tab, backward_tab = call(
        sort_tiles,
        (sds(1, TAB, jnp.int32), sds(1, BACKWARD_TAB, jnp.int32)),
        [VMEM, VMEM, SMEM],
    )(tile_rows[0], tile_cols[0], tile_count)
    half = jax.ShapeDtypeStruct((33, B, B), F32)
    tiles, acc0, acc1 = call(
        hold,
        (jax.ShapeDtypeStruct((128, B, B), BF16), half, half),
        [ANY],
        [pltpu.SemaphoreType.DMA((8,))],
        limit=43,
    )(adj)
    xs = (features, x3, x2, x1)
    scratch = [pltpu.VMEM((8, B, B), BF16), pltpu.SemaphoreType.DMA((2,))]
    _, other = call(
        functools.partial(forward_tiles, 0),
        (half, sds(4096)),
        [SMEM, ANY] + [VMEM] * 5,
        scratch,
        tiles=64,
        aliases={6: 0},
    )(forward_tab, *xs, tiles, acc0)
    got = lax.ppermute(other, "col", core_swap())
    acc = call(
        functools.partial(forward_tiles, 1),
        half,
        [SMEM, ANY] + [VMEM] * 5,
        scratch,
        aliases={6: 0},
    )(forward_tab, *xs, tiles, acc1)
    ms = call(core_sum, (sds(1024, dtype=F32),) + (sds(1024),) * 3, [VMEM] * 2)(acc, got)
    r1, r3, r2 = permute([ms[d] for d in ORDER], "col", [col_shift(True, d) for d in ORDER])
    total, msg = call(first_sum, (sds(1024, dtype=F32), sds(1536)), [VMEM] * 5)(
        ms[0], r1, r2, r3, cotangent
    )
    r1, r3, r2 = permute([msg] * 3, "col", [col_shift(False, d) for d in ORDER])
    act, msg = call(local, (sds(256, 256), sds(1024 + TAIL)), [VMEM] * 7)(
        total, r1, r2, r3, weight, bias_vector.reshape(1, 256), cotangent
    )
    r1, r3, r2 = permute([msg] * 3, "col", [col_shift(True, d) for d in ORDER])
    mine = (msg, r3, r2, r1)
    theirs = [lax.ppermute(m, "col", core_swap()) for m in mine]
    out, tail = sds(256 + TAIL), sds(TAIL, dtype=F32)
    sums = jax.ShapeDtypeStruct((9, B, B), F32)
    blocks, acc = pltpu.VMEM((64, B, B), BF16), pltpu.VMEM((9, B, B), F32)

    def backward(key, places, outs, scratch, tiles, aliases, *extra):
        pieces = [(mine + tuple(theirs))[p] for p in places]
        return call(
            functools.partial(backward_tiles, key, places),
            outs,
            [SMEM] + [VMEM] * (1 + len(places) + len(extra)),
            scratch,
            tiles=tiles,
            aliases=aliases,
        )(backward_tab, adj, *pieces, *extra)

    state = backward(0, (0, 2, 3), (sums, tail), [blocks], 48, None)
    state = backward(1, (1, 4, 6, 7), (sums, tail), [blocks], 64, {6: 0}, *state)
    ms = backward(2, (5,), (out,) * 3, [acc, blocks], 16, None, *state)
    (m,) = backward(3, (5,), (sds(256 + TAIL, dtype=F32),), [acc, blocks], 0, None, *state)
    ms = [ms[d - 1] for d in ORDER]
    rs = [lax.ppermute(a, "row", row_shift(d)) for a, d in zip(ms, ORDER)]
    feat, wgrad, bgrad = call(
        last_sum, (sds(256, 128), sds(128, 256, F32), sds(1, 256, F32)), [VMEM] * 4
    )(m, *rs)
    return (act, feat, wgrad, bgrad.reshape(256))


def solution(mesh):
    placed = (
        P(("row", "col"), None),
        P(),
        P(),
        P("row", "col", None, None, None),
        P("row", "col", None),
        P("row", "col", None),
        P("row", "col"),
        P(("row", "col"), None),
    )
    return jax.shard_map(
        on_device,
        mesh=mesh,
        in_specs=placed,
        out_specs=(P(("row", "col"), None), P(("row", "col"), None), P(), P()),
        check_vma=False,
    )
```

```python
import functools

import jax
import jax.numpy as jnp
from jax import lax
from jax.experimental import pallas as pl
from jax.experimental.pallas import tpu as pltpu
from jax.sharding import PartitionSpec as P

F32 = jnp.float32
BF16 = jnp.bfloat16
B = 128
VMEM = pl.BlockSpec(memory_space=pltpu.VMEM)
SMEM = pl.BlockSpec(memory_space=pltpu.SMEM)
ANY = pl.BlockSpec(memory_space=pl.ANY)
TAIL = 272
UNROLL = 16
WIDTH = 144
TAB = 384
BACKWARD_TAB = 640


def at(y, z, core):
    return (y * 4 + z) * 2 + core


def ring_of(y, z, core):
    return (core + y + z) % 2


def col_shift(first, d):
    pairs = []
    for y in range(4):
        for z in range(4):
            for core in range(2):
                ring = ring_of(y, z, core)
                along_z = (ring == 0) == first
                to_y, to_z = (y, (z + d) % 4) if along_z else ((y + d) % 4, z)
                pairs.append((at(y, z, core), at(to_y, to_z, ring_of(to_y, to_z, ring))))
    return pairs


def core_swap():
    return [(c, c ^ 1) for c in range(32)]


def row_shift(d):
    return [(r, (r + d) % 4) for r in range(4)]


def call(kernel, outs, ins, scratch=(), tiles=0, nbytes=0, aliases=None, limit=24):
    return pl.pallas_call(
        kernel,
        out_shape=outs,
        in_specs=ins,
        out_specs=jax.tree.map(lambda _: VMEM, outs),
        scratch_shapes=list(scratch),
        input_output_aliases=aliases or {},
        compiler_params=pltpu.CompilerParams(vmem_limit_bytes=limit * 2**20),
        cost_estimate=pl.CostEstimate(
            flops=2 * tiles * B**3, bytes_accessed=nbytes + tiles * 2**16, transcendentals=0
        ),
    )


def sds(rows, cols=B, dtype=BF16):
    return jax.ShapeDtypeStruct((rows, cols), dtype)


def permute(arrays, axis, pairs, together=True):
    arrays = lax.optimization_barrier(tuple(arrays))
    moved = [lax.ppermute(a, axis, p) for a, p in zip(arrays, pairs)]
    return lax.optimization_barrier(moved) if together else moved


ORDER = (1, 3, 2)


def sort_tiles(rows, cols, count, forward_tab, backward_tab):
    r, c = lax.axis_index("row"), lax.axis_index("col")
    core, z, y = c % 2, (c // 2) % 4, c // 8
    rows, cols = rows[...], cols[...]
    owner, sub = rows // 2, rows % 2
    core_to, z_to, y_to = owner % 2, (owner // 2) % 4, owner // 8
    dz, dy = (z_to - z + 4) % 4, (y_to - y + 4) % 4
    ring_to = ring_of(y_to, z_to, core_to)
    first = jnp.where(ring_to == 0, dz, dy)
    second = jnp.where(ring_to == 0, dy, dz)
    pos = (first * 4 + second) * 2 + sub
    half = (ring_to != ring_of(y, z, core)).astype(jnp.int32)
    ahead = (cols // 2 - r + 4) % 4
    slot = lax.broadcasted_iota(jnp.int32, (1, 128), 1)

    def table(key, keys, take, to, pad, width):
        key = jnp.where(slot < count[0, 0], key, keys)
        is_key = [jnp.where(key == k, 1.0, 0.0) for k in range(keys)]
        is_key = jnp.concatenate(is_key + [jnp.zeros((8 - keys, 128), F32)]).astype(BF16)
        low = lax.broadcasted_iota(jnp.int32, (128, 128), 0)
        high = lax.broadcasted_iota(jnp.int32, (128, 128), 1)
        before = jnp.where(low < high, 1.0, 0.0).astype(BF16)
        rank = jnp.dot(is_key, before, preferred_element_type=F32)
        place = jnp.full((1, 128), -1.0, F32)
        for k in range(keys):
            place = jnp.where(key == k, rank[k : k + 1] + float(k * WIDTH), place)
        place = jnp.broadcast_to(place, (8, 128)).T[:, 0:1].astype(jnp.int32)
        spots = lax.broadcasted_iota(jnp.int32, (128, width), 1)
        at_spot = jnp.where(place == spots, 1.0, 0.0).astype(BF16)
        fields = [slot.astype(F32), take.astype(F32), to.astype(F32), jnp.ones((1, 128), F32)]
        fields = jnp.concatenate(fields + [jnp.zeros((4, 128), F32)]).astype(BF16)
        found = jnp.dot(fields, at_spot, preferred_element_type=F32).astype(jnp.int32)
        entry = found[0:1] + found[1:2] * 2**8 + found[2:3] * 2**16
        entry = jnp.where(found[3:4] > 0, entry, pad * 2**16)
        total = jnp.sum(is_key.astype(F32), axis=1, keepdims=True).astype(jnp.int32)
        for k in range(keys):
            groups = (total[k : k + 1] + (UNROLL - 1)) // UNROLL
            entry = jnp.where(spots[0:1] == keys * WIDTH + k, groups, entry)
        return entry

    forward_tab[...] = table(1 - half, 2, ahead * 2 + cols % 2, pos, 32, TAB)
    late = ((first == 1) | (first == 2)).astype(jnp.int32)
    group = late + jnp.where(first == 0, 0, half)
    key = jnp.where(group < 2, group, jnp.where(ahead == 0, 3, 2))
    take = half * 32 + pos
    backward_tab[...] = table(key, 4, take, ahead * 2 + cols % 2, 8, BACKWARD_TAB)


def hold(adj, tiles, acc0, acc1, sem):
    n = sem.shape[0]
    parts = [pl.ds(k * (128 // n), 128 // n) for k in range(n)]
    copies = [
        pltpu.make_async_copy(adj.at[part], tiles.at[part], sem.at[k])
        for k, part in enumerate(parts)
    ]
    for copy in copies:
        copy.start()

    def block(i, _):
        acc0[i] = jnp.zeros((B, B), F32)
        acc1[i] = jnp.zeros((B, B), F32)
        return 0

    lax.fori_loop(0, 32, block, 0, unroll=4)
    for copy in copies:
        copy.wait()


def each_tile(tab, key, keys, adj, product, acc):
    def body(g, _):
        parts = []
        for u in range(UNROLL):
            e = tab[0, key * WIDTH + g * UNROLL + u]
            parts.append((product(adj[e & 127], (e >> 8) & 63), e >> 16))
        for part, to in parts:
            acc[to] += part
        return 0

    lax.fori_loop(0, tab[0, keys * WIDTH + key], body, 0)


def load_blocks(refs, rows, to):
    for k, ref in enumerate(refs):
        for i in range(rows // B):
            to[k * (rows // B) + i] = ref[i * B : (i + 1) * B]


def forward_tiles(key, tab, x0, x1, x2, x3, adj, _, acc, *refs):
    *out, xs, sem = refs
    copies = [
        pltpu.make_async_copy(x0.at[pl.ds(k * B, B)], xs.at[k], sem.at[k]) for k in range(2)
    ]
    for copy in copies:
        copy.start()
    load_blocks([x1, x2, x3], 256, xs.at[pl.ds(2, 6)])
    for copy in copies:
        copy.wait()
    each_tile(tab, key, 2, adj, lambda t, i: jnp.dot(t, xs[i], preferred_element_type=F32), acc)
    if key == 0:

        def store(i, _):
            out[0][pl.ds(pl.multiple_of(i * B, B), B)] = acc[i].astype(BF16)
            return 0

        lax.fori_loop(0, 32, store, 0, unroll=4)


def core_sum(acc, got, m0, m1, m2, m3):
    for k, m in enumerate((m0, m1, m2, m3)):
        for i in range(8):
            rows = pl.ds((k * 8 + i) * B, B)
            total = acc[k * 8 + i] + got[rows].astype(F32)
            m[i * B : (i + 1) * B] = total.astype(m.dtype)


def first_sum(m0, r1, r2, r3, cot, total, msg):
    for i in range(0, 1024, 256):
        rows = pl.ds(i, 256)
        t = m0[rows] + (r1[rows].astype(F32) + r2[rows].astype(F32) + r3[rows].astype(F32))
        total[rows] = t
        msg[rows] = t.astype(BF16)
    msg[1024:1280] = cot[:, 0:B]
    msg[1280:1536] = cot[:, B : 2 * B]


def put_tail(msg, base, wg, bg):
    msg[pl.ds(base, 256)] = wg.astype(msg.dtype)
    if msg.dtype == F32:
        msg[pl.ds(base + 256, 16)] = jnp.concatenate([bg, jnp.zeros((14, B), F32)])
    else:
        high = bg.astype(BF16).astype(F32)
        low = bg - high
        block = jnp.concatenate([high, low, jnp.zeros((12, B), F32)])
        msg[pl.ds(base + 256, 16)] = block.astype(BF16)


def get_tail(msg, base):
    wg = msg[pl.ds(base, 256)].astype(F32)
    block = msg[pl.ds(base + 256, 16)].astype(F32)
    return wg, block[0:2] + block[2:4]


def local(s0, r1, r2, r3, weight, bias, cot, act, msg):
    w = weight[...]
    over_nodes = (((0,), (0,)), ((), ()))
    wg, bg = jnp.zeros((B, 256), F32), jnp.zeros((1, 256), F32)
    for k, r in enumerate((None, r3, r2, r1)):
        if k == 0:
            c = cot[...]
        else:
            c = jnp.concatenate([r[1024:1280], r[1280:1536]], axis=1)
        y = s0[pl.ds(k * 256, 256)]
        for d, r in ((1, r1), (2, r2), (3, r3)):
            y += r[pl.ds((k + d) % 4 * 256, 256)].astype(F32)
        y_high = y.astype(BF16)
        y_low = (y - y_high.astype(F32)).astype(BF16)
        summed = jnp.dot(y_high, w, preferred_element_type=F32) + jnp.dot(
            y_low, w, preferred_element_type=F32
        )
        pre = summed + bias[...]
        sig = jax.nn.sigmoid(pre)
        if k == 0:
            act[...] = (pre * sig).astype(BF16)
        slope = sig * (1.0 + pre * (1.0 - sig))
        grad = (c.astype(F32) * slope).astype(BF16)
        g = lax.dot_general(w, grad, (((1,), (1,)), ((), ())), preferred_element_type=F32)
        g = g.astype(BF16)
        msg[pl.ds(k * 256, B)] = g[:, 0:B]
        msg[pl.ds(k * 256 + B, B)] = g[:, B : 2 * B]
        wg += lax.dot_general(y_high, grad, over_nodes, preferred_element_type=F32)
        wg += lax.dot_general(y_low, grad, over_nodes, preferred_element_type=F32)
        bg += jnp.sum(grad.astype(F32), axis=0, keepdims=True)
    put_tail(
        msg,
        1024,
        jnp.concatenate([wg[:, 0:B], wg[:, B : 2 * B]]),
        jnp.concatenate([bg[:, 0:B], bg[:, B : 2 * B]]),
    )


def sum_tails(pieces):
    wg, bg = get_tail(pieces[0], 1024)
    for piece in pieces[1:]:
        wg_r, bg_r = get_tail(piece, 1024)
        wg += wg_r
        bg += bg_r
    return wg, bg


def backward_tiles(key, places, tab, adj, *refs):
    def product(t, i):
        return jnp.dot(gs[i], t, preferred_element_type=F32)

    pieces, refs, gs = refs[: len(places)], refs[len(places) : -1], refs[-1]
    for place, piece in zip(places, pieces):
        load_blocks([piece], 1024, gs.at[pl.ds(place * 8, 8)])
    if key < 2:
        if key == 0:
            acc, tail = refs
            acc[...] = jnp.zeros((9, B, B), F32)
        else:
            _, tail_in, acc, tail = refs
        each_tile(tab, key, 4, adj, product, acc)
        wg, bg = sum_tails(pieces)
        if key == 1:
            wg, bg = wg + tail_in[0:256], bg + tail_in[256:258]
        put_tail(tail, 0, wg, bg)
        return
    acc_in, tail_in, *outs, acc = refs
    first = 2 if key == 2 else 0
    last = first + 2 * len(outs)
    acc[first:last] = acc_in[first:last]
    each_tile(tab, key, 4, adj, product, acc)
    wg, bg = sum_tails(pieces)
    wg, bg = wg + tail_in[0:256], bg + tail_in[256:258]
    for k, m in enumerate(outs):
        m[0:B] = acc[first + 2 * k].astype(m.dtype)
        m[B : 2 * B] = acc[first + 2 * k + 1].astype(m.dtype)
        put_tail(m, 256, wg, bg)


def last_sum(m0, r1, r2, r3, feat, wgrad, bgrad):
    for k in range(2):
        rows = pl.ds(k * B, B)
        total = m0[rows] + (r1[rows].astype(F32) + r2[rows].astype(F32) + r3[rows].astype(F32))
        feat[rows] = total.T.astype(BF16)
    wg, block = m0[pl.ds(256, 256)], m0[pl.ds(512, 16)]
    bg = block[0:2]
    for r in (r1, r2, r3):
        wg_r, bg_r = get_tail(r, 256)
        wg += wg_r
        bg += bg_r
    wgrad[:, 0:B] = wg[0:B]
    wgrad[:, B : 2 * B] = wg[B : 2 * B]
    bgrad[:, 0:B] = bg[0:1]
    bgrad[:, B : 2 * B] = bg[1:2]


def on_device(
    features, weight, bias_vector, adjacency, tile_rows, tile_cols, tile_count, cotangent
):
    adj = adjacency[0, 0]
    x1, x3, x2 = permute([features] * 3, "row", [row_shift(d) for d in ORDER])
    forward_tab, backward_tab = call(
        sort_tiles,
        (sds(1, TAB, jnp.int32), sds(1, BACKWARD_TAB, jnp.int32)),
        [VMEM, VMEM, SMEM],
    )(tile_rows[0], tile_cols[0], tile_count)
    half = jax.ShapeDtypeStruct((33, B, B), F32)
    tiles, acc0, acc1 = call(
        hold,
        (jax.ShapeDtypeStruct((128, B, B), BF16), half, half),
        [ANY],
        [pltpu.SemaphoreType.DMA((8,))],
        limit=43,
    )(adj)
    xs = (features, x3, x2, x1)
    scratch = [pltpu.VMEM((8, B, B), BF16), pltpu.SemaphoreType.DMA((2,))]
    _, other = call(
        functools.partial(forward_tiles, 0),
        (half, sds(4096)),
        [SMEM, ANY] + [VMEM] * 5,
        scratch,
        tiles=64,
        aliases={6: 0},
    )(forward_tab, *xs, tiles, acc0)
    got = lax.ppermute(other, "col", core_swap())
    acc = call(
        functools.partial(forward_tiles, 1),
        half,
        [SMEM, ANY] + [VMEM] * 5,
        scratch,
        aliases={6: 0},
    )(forward_tab, *xs, tiles, acc1)
    ms = call(core_sum, (sds(1024, dtype=F32),) + (sds(1024),) * 3, [VMEM] * 2)(acc, got)
    r1, r3, r2 = permute([ms[d] for d in ORDER], "col", [col_shift(True, d) for d in ORDER])
    total, msg = call(first_sum, (sds(1024, dtype=F32), sds(1536)), [VMEM] * 5)(
        ms[0], r1, r2, r3, cotangent
    )
    r1, r3, r2 = permute([msg] * 3, "col", [col_shift(False, d) for d in ORDER])
    act, msg = call(local, (sds(256, 256), sds(1024 + TAIL)), [VMEM] * 7)(
        total, r1, r2, r3, weight, bias_vector.reshape(1, 256), cotangent
    )
    r1, r3, r2 = permute([msg] * 3, "col", [col_shift(True, d) for d in ORDER], False)
    mine = [msg, r3, r2, r1]
    theirs = [None] * 4
    for k in (0, 3):
        theirs[k] = lax.ppermute(mine[k], "col", core_swap())
    out, tail = sds(256 + TAIL), sds(TAIL, dtype=F32)
    sums = jax.ShapeDtypeStruct((9, B, B), F32)
    blocks, acc = pltpu.VMEM((64, B, B), BF16), pltpu.VMEM((9, B, B), F32)

    def backward(key, places, outs, scratch, tiles, aliases, *extra):
        pieces = [(mine + theirs)[p] for p in places]
        return call(
            functools.partial(backward_tiles, key, places),
            outs,
            [SMEM] + [VMEM] * (1 + len(places) + len(extra)),
            scratch,
            tiles=tiles,
            aliases=aliases,
        )(backward_tab, adj, *pieces, *extra)

    state = backward(0, (0, 3, 4), (sums, tail), [blocks], 48, None)
    mine[1], mine[2], *state = lax.optimization_barrier((mine[1], mine[2], *state))
    for k in (1, 2):
        theirs[k] = lax.ppermute(mine[k], "col", core_swap())
    state = backward(1, (1, 2, 7), (sums, tail), [blocks], 48, {5: 0}, *state)
    ms = backward(2, (5, 6), (out,) * 3, [acc, blocks], 16, None, *state)
    (m,) = backward(3, (5, 6), (sds(256 + TAIL, dtype=F32),), [acc, blocks], 0, None, *state)
    ms = [ms[d - 1] for d in ORDER]
    rs = [lax.ppermute(a, "row", row_shift(d)) for a, d in zip(ms, ORDER)]
    feat, wgrad, bgrad = call(
        last_sum, (sds(256, 128), sds(128, 256, F32), sds(1, 256, F32)), [VMEM] * 4
    )(m, *rs)
    return (act, feat, wgrad, bgrad.reshape(256))


def solution(mesh):
    placed = (
        P(("row", "col"), None),
        P(),
        P(),
        P("row", "col", None, None, None),
        P("row", "col", None),
        P("row", "col", None),
        P("row", "col"),
        P(("row", "col"), None),
    )
    return jax.shard_map(
        on_device,
        mesh=mesh,
        in_specs=placed,
        out_specs=(P(("row", "col"), None), P(("row", "col"), None), P(), P()),
        check_vma=False,
    )
```

```python
import functools

import jax
import jax.numpy as jnp
from jax import lax
from jax.experimental import pallas as pl
from jax.experimental.pallas import tpu as pltpu
from jax.sharding import PartitionSpec as P

F32 = jnp.float32
BF16 = jnp.bfloat16
B = 128
VMEM = pl.BlockSpec(memory_space=pltpu.VMEM)
SMEM = pl.BlockSpec(memory_space=pltpu.SMEM)
ANY = pl.BlockSpec(memory_space=pl.ANY)
TAIL = 272
UNROLL = 16
WIDTH = 144
TAB = 384
BACKWARD_TAB = 640


def at(y, z, core):
    return (y * 4 + z) * 2 + core


def ring_of(y, z, core):
    return (core + y + z) % 2


def col_shift(first, d):
    pairs = []
    for y in range(4):
        for z in range(4):
            for core in range(2):
                ring = ring_of(y, z, core)
                along_z = (ring == 0) == first
                to_y, to_z = (y, (z + d) % 4) if along_z else ((y + d) % 4, z)
                pairs.append((at(y, z, core), at(to_y, to_z, ring_of(to_y, to_z, ring))))
    return pairs


def core_swap():
    return [(c, c ^ 1) for c in range(32)]


def row_shift(d):
    return [(r, (r + d) % 4) for r in range(4)]


def call(kernel, outs, ins, scratch=(), tiles=0, nbytes=0, aliases=None, limit=24):
    return pl.pallas_call(
        kernel,
        out_shape=outs,
        in_specs=ins,
        out_specs=jax.tree.map(lambda _: VMEM, outs),
        scratch_shapes=list(scratch),
        input_output_aliases=aliases or {},
        compiler_params=pltpu.CompilerParams(vmem_limit_bytes=limit * 2**20),
        cost_estimate=pl.CostEstimate(
            flops=2 * tiles * B**3, bytes_accessed=nbytes + tiles * 2**16, transcendentals=0
        ),
    )


def sds(rows, cols=B, dtype=BF16):
    return jax.ShapeDtypeStruct((rows, cols), dtype)


def permute(arrays, axis, pairs, together=True):
    arrays = lax.optimization_barrier(tuple(arrays))
    moved = [lax.ppermute(a, axis, p) for a, p in zip(arrays, pairs)]
    return lax.optimization_barrier(moved) if together else moved


ORDER = (1, 3, 2)
FAR_FIRST = (2, 1, 3)


def sort_tiles(rows, cols, count, forward_tab, backward_tab):
    r, c = lax.axis_index("row"), lax.axis_index("col")
    core, z, y = c % 2, (c // 2) % 4, c // 8
    rows, cols = rows[...], cols[...]
    owner, sub = rows // 2, rows % 2
    core_to, z_to, y_to = owner % 2, (owner // 2) % 4, owner // 8
    dz, dy = (z_to - z + 4) % 4, (y_to - y + 4) % 4
    ring_to = ring_of(y_to, z_to, core_to)
    first = jnp.where(ring_to == 0, dz, dy)
    second = jnp.where(ring_to == 0, dy, dz)
    pos = (first * 4 + second) * 2 + sub
    half = (ring_to != ring_of(y, z, core)).astype(jnp.int32)
    ahead = (cols // 2 - r + 4) % 4
    slot = lax.broadcasted_iota(jnp.int32, (1, 128), 1)

    def table(key, keys, take, to, pad, width):
        key = jnp.where(slot < count[...], key, keys)
        is_key = [jnp.where(key == k, 1.0, 0.0) for k in range(keys)]
        is_key = jnp.concatenate(is_key + [jnp.zeros((8 - keys, 128), F32)]).astype(BF16)
        low = lax.broadcasted_iota(jnp.int32, (128, 128), 0)
        high = lax.broadcasted_iota(jnp.int32, (128, 128), 1)
        before = jnp.where(low < high, 1.0, 0.0).astype(BF16)
        rank = jnp.dot(is_key, before, preferred_element_type=F32)
        place = jnp.full((1, 128), -1.0, F32)
        for k in range(keys):
            place = jnp.where(key == k, rank[k : k + 1] + float(k * WIDTH), place)
        place = jnp.broadcast_to(place, (8, 128)).T[:, 0:1].astype(jnp.int32)
        spots = lax.broadcasted_iota(jnp.int32, (128, width), 1)
        at_spot = jnp.where(place == spots, 1.0, 0.0).astype(BF16)
        fields = [slot.astype(F32), take.astype(F32), to.astype(F32), jnp.ones((1, 128), F32)]
        fields = jnp.concatenate(fields + [jnp.zeros((4, 128), F32)]).astype(BF16)
        found = jnp.dot(fields, at_spot, preferred_element_type=F32).astype(jnp.int32)
        entry = found[0:1] + found[1:2] * 2**8 + found[2:3] * 2**16
        entry = jnp.where(found[3:4] > 0, entry, pad * 2**16)
        total = jnp.sum(is_key.astype(F32), axis=1, keepdims=True).astype(jnp.int32)
        for k in range(keys):
            groups = (total[k : k + 1] + (UNROLL - 1)) // UNROLL
            entry = jnp.where(spots[0:1] == keys * WIDTH + k, groups, entry)
        return entry

    forward_tab[...] = table(1 - half, 2, ahead * 2 + cols % 2, pos, 32, TAB)
    late = ((first == 1) | (first == 2)).astype(jnp.int32)
    group = late + jnp.where(first == 0, 0, half)
    key = jnp.where(group < 2, group, jnp.where(ahead == 0, 3, 2))
    take = half * 32 + pos
    backward_tab[...] = table(key, 4, take, ahead * 2 + cols % 2, 8, BACKWARD_TAB)


def hold(adj, tiles, acc0, acc1, sem):
    n = sem.shape[0]
    parts = [pl.ds(k * (128 // n), 128 // n) for k in range(n)]
    copies = [
        pltpu.make_async_copy(adj.at[part], tiles.at[part], sem.at[k])
        for k, part in enumerate(parts)
    ]
    for copy in copies:
        copy.start()

    def block(i, _):
        acc0[i] = jnp.zeros((B, B), F32)
        acc1[i] = jnp.zeros((B, B), F32)
        return 0

    lax.fori_loop(0, 32, block, 0, unroll=4)
    for copy in copies:
        copy.wait()


def each_tile(tab, key, keys, adj, product, acc):
    def body(g, _):
        parts = []
        for u in range(UNROLL):
            e = tab[0, key * WIDTH + g * UNROLL + u]
            parts.append((product(adj[e & 127], (e >> 8) & 63), e >> 16))
        for part, to in parts:
            acc[to] += part
        return 0

    lax.fori_loop(0, tab[0, keys * WIDTH + key], body, 0)


def load_blocks(refs, rows, to):
    for k, ref in enumerate(refs):
        for i in range(rows // B):
            to[k * (rows // B) + i] = ref[i * B : (i + 1) * B]


def forward_tiles(key, tab, x0, x1, x2, x3, adj, _, acc, *refs):
    *out, xs = refs
    load_blocks([x0, x1, x2, x3], 256, xs)
    each_tile(tab, key, 2, adj, lambda t, i: jnp.dot(t, xs[i], preferred_element_type=F32), acc)
    if key == 0:

        def store(i, _):
            out[0][pl.ds(pl.multiple_of(i * B, B), B)] = acc[i].astype(BF16)
            return 0

        lax.fori_loop(0, 32, store, 0, unroll=4)


def core_sum(acc, got, m0, m1, m2, m3):
    for k, m in enumerate((m0, m1, m2, m3)):
        for i in range(8):
            rows = pl.ds((k * 8 + i) * B, B)
            total = acc[k * 8 + i] + got[rows].astype(F32)
            m[i * B : (i + 1) * B] = total.astype(m.dtype)


def first_sum(m0, r1, r2, r3, cot, total, msg):
    for i in range(0, 1024, 256):
        rows = pl.ds(i, 256)
        t = m0[rows] + (r1[rows].astype(F32) + r2[rows].astype(F32) + r3[rows].astype(F32))
        total[rows] = t
        msg[rows] = t.astype(BF16)
    msg[1024:1280] = cot[:, 0:B]
    msg[1280:1536] = cot[:, B : 2 * B]


def put_tail(msg, base, wg, bg):
    msg[pl.ds(base, 256)] = wg.astype(msg.dtype)
    if msg.dtype == F32:
        msg[pl.ds(base + 256, 16)] = jnp.concatenate([bg, jnp.zeros((14, B), F32)])
    else:
        high = bg.astype(BF16).astype(F32)
        low = bg - high
        block = jnp.concatenate([high, low, jnp.zeros((12, B), F32)])
        msg[pl.ds(base + 256, 16)] = block.astype(BF16)


def get_tail(msg, base):
    wg = msg[pl.ds(base, 256)].astype(F32)
    block = msg[pl.ds(base + 256, 16)].astype(F32)
    return wg, block[0:2] + block[2:4]


def local(s0, r1, r2, r3, weight, bias, cot, act, msg):
    w = weight[...]
    over_nodes = (((0,), (0,)), ((), ()))
    wg, bg = jnp.zeros((B, 256), F32), jnp.zeros((1, 256), F32)
    for k, r in enumerate((None, r3, r2, r1)):
        if k == 0:
            c = cot[...]
        else:
            c = jnp.concatenate([r[1024:1280], r[1280:1536]], axis=1)
        y = s0[pl.ds(k * 256, 256)]
        for d, r in ((1, r1), (2, r2), (3, r3)):
            y += r[pl.ds((k + d) % 4 * 256, 256)].astype(F32)
        y_high = y.astype(BF16)
        y_low = (y - y_high.astype(F32)).astype(BF16)
        summed = jnp.dot(y_high, w, preferred_element_type=F32) + jnp.dot(
            y_low, w, preferred_element_type=F32
        )
        pre = summed + bias[...]
        sig = jax.nn.sigmoid(pre)
        if k == 0:
            act[...] = (pre * sig).astype(BF16)
        slope = sig * (1.0 + pre * (1.0 - sig))
        grad = (c.astype(F32) * slope).astype(BF16)
        g = lax.dot_general(w, grad, (((1,), (1,)), ((), ())), preferred_element_type=F32)
        g = g.astype(BF16)
        msg[pl.ds(k * 256, B)] = g[:, 0:B]
        msg[pl.ds(k * 256 + B, B)] = g[:, B : 2 * B]
        wg += lax.dot_general(y_high, grad, over_nodes, preferred_element_type=F32)
        wg += lax.dot_general(y_low, grad, over_nodes, preferred_element_type=F32)
        bg += jnp.sum(grad.astype(F32), axis=0, keepdims=True)
    put_tail(
        msg,
        1024,
        jnp.concatenate([wg[:, 0:B], wg[:, B : 2 * B]]),
        jnp.concatenate([bg[:, 0:B], bg[:, B : 2 * B]]),
    )


def sum_tails(pieces):
    wg, bg = get_tail(pieces[0], 1024)
    for piece in pieces[1:]:
        wg_r, bg_r = get_tail(piece, 1024)
        wg += wg_r
        bg += bg_r
    return wg, bg


def backward_tiles(key, places, tab, adj, *refs):
    def product(t, i):
        return jnp.dot(gs[i], t, preferred_element_type=F32)

    pieces, refs, gs = refs[: len(places)], refs[len(places) : -1], refs[-1]
    for place, piece in zip(places, pieces):
        load_blocks([piece], 1024, gs.at[pl.ds(place * 8, 8)])
    if key < 2:
        if key == 0:
            acc, tail = refs
            acc[...] = jnp.zeros((9, B, B), F32)
        else:
            _, tail_in, acc, tail = refs
        each_tile(tab, key, 4, adj, product, acc)
        wg, bg = sum_tails(pieces)
        if key == 1:
            wg, bg = wg + tail_in[0:256], bg + tail_in[256:258]
        put_tail(tail, 0, wg, bg)
        return
    acc_in, tail_in, *outs, acc = refs
    first = 2 if key == 2 else 0
    last = first + 2 * len(outs)
    acc[first:last] = acc_in[first:last]
    each_tile(tab, key, 4, adj, product, acc)
    wg, bg = sum_tails(pieces)
    wg, bg = wg + tail_in[0:256], bg + tail_in[256:258]
    for k, m in enumerate(outs):
        m[0:B] = acc[first + 2 * k].astype(m.dtype)
        m[B : 2 * B] = acc[first + 2 * k + 1].astype(m.dtype)
        put_tail(m, 256, wg, bg)


def last_sum(m0, r1, r2, r3, feat, wgrad, bgrad):
    for k in range(2):
        rows = pl.ds(k * B, B)
        total = m0[rows] + (r1[rows].astype(F32) + r2[rows].astype(F32) + r3[rows].astype(F32))
        feat[rows] = total.T.astype(BF16)
    wg, block = m0[pl.ds(256, 256)], m0[pl.ds(512, 16)]
    bg = block[0:2]
    for r in (r1, r2, r3):
        wg_r, bg_r = get_tail(r, 256)
        wg += wg_r
        bg += bg_r
    wgrad[:, 0:B] = wg[0:B]
    wgrad[:, B : 2 * B] = wg[B : 2 * B]
    bgrad[:, 0:B] = bg[0:1]
    bgrad[:, B : 2 * B] = bg[1:2]


def on_device(
    features, weight, bias_vector, adjacency, tile_rows, tile_cols, tile_count, cotangent
):
    adj = adjacency[0, 0]
    x1, x3, x2 = permute([features] * 3, "row", [row_shift(d) for d in ORDER])
    forward_tab, backward_tab = call(
        sort_tiles,
        (sds(1, TAB, jnp.int32), sds(1, BACKWARD_TAB, jnp.int32)),
        [VMEM] * 3,
    )(tile_rows[0], tile_cols[0], tile_count)
    half = jax.ShapeDtypeStruct((33, B, B), F32)
    tiles, acc0, acc1 = call(
        hold,
        (jax.ShapeDtypeStruct((128, B, B), BF16), half, half),
        [ANY],
        [pltpu.SemaphoreType.DMA((8,))],
        limit=43,
    )(adj)
    xs = (features, x3, x2, x1)
    scratch = [pltpu.VMEM((8, B, B), BF16)]
    _, other = call(
        functools.partial(forward_tiles, 0),
        (half, sds(4096)),
        [SMEM] + [VMEM] * 6,
        scratch,
        tiles=64,
        aliases={6: 0},
    )(forward_tab, *xs, tiles, acc0)
    got = lax.ppermute(other, "col", core_swap())
    acc = call(
        functools.partial(forward_tiles, 1),
        half,
        [SMEM] + [VMEM] * 6,
        scratch,
        aliases={6: 0},
    )(forward_tab, *xs, tiles, acc1)
    ms = call(core_sum, (sds(1024, dtype=F32),) + (sds(1024),) * 3, [VMEM] * 2)(acc, got)
    r2, r1, r3 = permute([ms[d] for d in FAR_FIRST], "col", [col_shift(True, d) for d in FAR_FIRST])
    total, msg = call(first_sum, (sds(1024, dtype=F32), sds(1536)), [VMEM] * 5)(
        ms[0], r1, r2, r3, cotangent
    )
    r2, r1, r3 = permute([msg] * 3, "col", [col_shift(False, d) for d in FAR_FIRST])
    act, msg = call(local, (sds(256, 256), sds(1024 + TAIL)), [VMEM] * 7)(
        total, r1, r2, r3, weight, bias_vector.reshape(1, 256), cotangent
    )
    r1, r3, r2 = permute([msg] * 3, "col", [col_shift(True, d) for d in ORDER], False)
    mine = [msg, r3, r2, r1]
    theirs = [None] * 4
    for k in (0, 3):
        theirs[k] = lax.ppermute(mine[k], "col", core_swap())
    out, tail = sds(256 + TAIL), sds(TAIL, dtype=F32)
    sums = jax.ShapeDtypeStruct((9, B, B), F32)
    blocks, acc = pltpu.VMEM((64, B, B), BF16), pltpu.VMEM((9, B, B), F32)

    def backward(key, places, outs, scratch, tiles, aliases, *extra):
        pieces = [(mine + theirs)[p] for p in places]
        return call(
            functools.partial(backward_tiles, key, places),
            outs,
            [SMEM] + [VMEM] * (1 + len(places) + len(extra)),
            scratch,
            tiles=tiles,
            aliases=aliases,
        )(backward_tab, adj, *pieces, *extra)

    state = backward(0, (0, 3, 4), (sums, tail), [blocks], 48, None)
    mine[1], mine[2], *state = lax.optimization_barrier((mine[1], mine[2], *state))
    for k in (1, 2):
        theirs[k] = lax.ppermute(mine[k], "col", core_swap())
    state = backward(1, (1, 2, 7), (sums, tail), [blocks], 48, {5: 0}, *state)
    ms = backward(2, (5, 6), (out,) * 3, [acc, blocks], 16, None, *state)
    (m,) = backward(3, (5, 6), (sds(256 + TAIL, dtype=F32),), [acc, blocks], 0, None, *state)
    ms = [ms[d - 1] for d in ORDER]
    rs = [lax.ppermute(a, "row", row_shift(d)) for a, d in zip(ms, ORDER)]
    feat, wgrad, bgrad = call(
        last_sum, (sds(256, 128), sds(128, 256, F32), sds(1, 256, F32)), [VMEM] * 4
    )(m, *rs)
    return (act, feat, wgrad, bgrad.reshape(256))


def solution(mesh):
    placed = (
        P(("row", "col"), None),
        P(),
        P(),
        P("row", "col", None, None, None),
        P("row", "col", None),
        P("row", "col", None),
        P("row", "col"),
        P(("row", "col"), None),
    )
    return jax.shard_map(
        on_device,
        mesh=mesh,
        in_specs=placed,
        out_specs=(P(("row", "col"), None), P(("row", "col"), None), P(), P()),
        check_vma=False,
    )
```

```python
import functools

import jax
import jax.numpy as jnp
from jax import lax
from jax.experimental import pallas as pl
from jax.experimental.pallas import tpu as pltpu
from jax.sharding import PartitionSpec as P

F32 = jnp.float32
BF16 = jnp.bfloat16
B = 128
VMEM = pl.BlockSpec(memory_space=pltpu.VMEM)
SMEM = pl.BlockSpec(memory_space=pltpu.SMEM)
ANY = pl.BlockSpec(memory_space=pl.ANY)
TAIL = 272
UNROLL = 16
WIDTH = 144
TAB = 384
BACKWARD_TAB = 640


def at(y, z, core):
    return (y * 4 + z) * 2 + core


def ring_of(y, z, core):
    return (core + y + z) % 2


def col_shift(first, d):
    pairs = []
    for y in range(4):
        for z in range(4):
            for core in range(2):
                ring = ring_of(y, z, core)
                along_z = (ring == 0) == first
                to_y, to_z = (y, (z + d) % 4) if along_z else ((y + d) % 4, z)
                pairs.append((at(y, z, core), at(to_y, to_z, ring_of(to_y, to_z, ring))))
    return pairs


def core_swap():
    return [(c, c ^ 1) for c in range(32)]


def row_shift(d):
    return [(r, (r + d) % 4) for r in range(4)]


def call(kernel, outs, ins, scratch=(), tiles=0, nbytes=0, aliases=None, limit=24):
    return pl.pallas_call(
        kernel,
        out_shape=outs,
        in_specs=ins,
        out_specs=jax.tree.map(lambda _: VMEM, outs),
        scratch_shapes=list(scratch),
        input_output_aliases=aliases or {},
        compiler_params=pltpu.CompilerParams(vmem_limit_bytes=limit * 2**20),
        cost_estimate=pl.CostEstimate(
            flops=2 * tiles * B**3, bytes_accessed=nbytes + tiles * 2**16, transcendentals=0
        ),
    )


def sds(rows, cols=B, dtype=BF16):
    return jax.ShapeDtypeStruct((rows, cols), dtype)


def permute(arrays, axis, pairs, together=True):
    arrays = lax.optimization_barrier(tuple(arrays))
    moved = [lax.ppermute(a, axis, p) for a, p in zip(arrays, pairs)]
    return lax.optimization_barrier(moved) if together else moved


ORDER = (1, 3, 2)
FAR_FIRST = (2, 1, 3)


def sort_tiles(rows, cols, count, forward_tab, backward_tab):
    r, c = lax.axis_index("row"), lax.axis_index("col")
    core, z, y = c % 2, (c // 2) % 4, c // 8
    rows, cols = rows[...], cols[...]
    owner, sub = rows // 2, rows % 2
    core_to, z_to, y_to = owner % 2, (owner // 2) % 4, owner // 8
    dz, dy = (z_to - z + 4) % 4, (y_to - y + 4) % 4
    ring_to = ring_of(y_to, z_to, core_to)
    first = jnp.where(ring_to == 0, dz, dy)
    second = jnp.where(ring_to == 0, dy, dz)
    pos = (first * 4 + second) * 2 + sub
    half = (ring_to != ring_of(y, z, core)).astype(jnp.int32)
    ahead = (cols // 2 - r + 4) % 4
    slot = lax.broadcasted_iota(jnp.int32, (1, 128), 1)

    def table(key, keys, take, to, pad, width):
        key = jnp.where(slot < count[...], key, keys)
        is_key = [jnp.where(key == k, 1.0, 0.0) for k in range(keys)]
        is_key = jnp.concatenate(is_key + [jnp.zeros((8 - keys, 128), F32)]).astype(BF16)
        low = lax.broadcasted_iota(jnp.int32, (128, 128), 0)
        high = lax.broadcasted_iota(jnp.int32, (128, 128), 1)
        before = jnp.where(low < high, 1.0, 0.0).astype(BF16)
        rank = jnp.dot(is_key, before, preferred_element_type=F32)
        place = jnp.full((1, 128), -1.0, F32)
        for k in range(keys):
            place = jnp.where(key == k, rank[k : k + 1] + float(k * WIDTH), place)
        place = jnp.broadcast_to(place, (8, 128)).T[:, 0:1].astype(jnp.int32)
        spots = lax.broadcasted_iota(jnp.int32, (128, width), 1)
        at_spot = jnp.where(place == spots, 1.0, 0.0).astype(BF16)
        fields = [slot.astype(F32), take.astype(F32), to.astype(F32), jnp.ones((1, 128), F32)]
        fields = jnp.concatenate(fields + [jnp.zeros((4, 128), F32)]).astype(BF16)
        found = jnp.dot(fields, at_spot, preferred_element_type=F32).astype(jnp.int32)
        entry = found[0:1] + found[1:2] * 2**8 + found[2:3] * 2**16
        entry = jnp.where(found[3:4] > 0, entry, pad * 2**16)
        total = jnp.sum(is_key.astype(F32), axis=1, keepdims=True).astype(jnp.int32)
        for k in range(keys):
            groups = (total[k : k + 1] + (UNROLL - 1)) // UNROLL
            entry = jnp.where(spots[0:1] == keys * WIDTH + k, groups, entry)
        return entry

    forward_tab[...] = table(1 - half, 2, ahead * 2 + cols % 2, pos, 32, TAB)
    late = ((first == 1) | (first == 2)).astype(jnp.int32)
    group = late + jnp.where(first == 0, 0, half)
    key = jnp.where(group < 2, group, jnp.where(ahead == 0, 3, 2))
    take = half * 32 + pos
    backward_tab[...] = table(key, 4, take, ahead * 2 + cols % 2, 8, BACKWARD_TAB)


def hold(adj, tiles, acc0, acc1, sem):
    n = sem.shape[0]
    parts = [pl.ds(k * (128 // n), 128 // n) for k in range(n)]
    copies = [
        pltpu.make_async_copy(adj.at[part], tiles.at[part], sem.at[k])
        for k, part in enumerate(parts)
    ]
    for copy in copies:
        copy.start()

    def block(i, _):
        acc0[i] = jnp.zeros((B, B), F32)
        acc1[i] = jnp.zeros((B, B), F32)
        return 0

    lax.fori_loop(0, 32, block, 0, unroll=4)
    for copy in copies:
        copy.wait()


def each_tile(tab, key, keys, adj, product, acc):
    def body(g, _):
        parts = []
        for u in range(UNROLL):
            e = tab[0, key * WIDTH + g * UNROLL + u]
            parts.append((product(adj[e & 127], (e >> 8) & 63), e >> 16))
        for part, to in parts:
            acc[to] += part
        return 0

    lax.fori_loop(0, tab[0, keys * WIDTH + key], body, 0)


def load_blocks(refs, rows, to):
    for k, ref in enumerate(refs):
        for i in range(rows // B):
            to[k * (rows // B) + i] = ref[i * B : (i + 1) * B]


def forward_tiles(key, tab, x0, x1, x2, x3, adj, _, acc, *refs):
    *out, xs = refs
    load_blocks([x0, x1, x2, x3], 256, xs)
    each_tile(tab, key, 2, adj, lambda t, i: jnp.dot(t, xs[i], preferred_element_type=F32), acc)
    if key == 0:

        def store(i, _):
            out[0][pl.ds(pl.multiple_of(i * B, B), B)] = acc[i].astype(BF16)
            return 0

        lax.fori_loop(0, 32, store, 0, unroll=4)


def core_sum(acc, got, m0, m1, m2, m3):
    for k, m in enumerate((m0, m1, m2, m3)):
        for i in range(8):
            rows = pl.ds((k * 8 + i) * B, B)
            total = acc[k * 8 + i] + got[rows].astype(F32)
            m[i * B : (i + 1) * B] = total.astype(m.dtype)


def first_sum(m0, r1, r2, r3, cot, total, msg):
    for i in range(0, 1024, 256):
        rows = pl.ds(i, 256)
        t = m0[rows] + (r1[rows].astype(F32) + r2[rows].astype(F32) + r3[rows].astype(F32))
        total[rows] = t
        msg[rows] = t.astype(BF16)
    msg[1024:1280] = cot[:, 0:B]
    msg[1280:1536] = cot[:, B : 2 * B]


def put_tail(msg, base, wg, bg):
    msg[pl.ds(base, 256)] = wg.astype(msg.dtype)
    if msg.dtype == F32:
        msg[pl.ds(base + 256, 16)] = jnp.concatenate([bg, jnp.zeros((14, B), F32)])
    else:
        high = bg.astype(BF16).astype(F32)
        low = bg - high
        block = jnp.concatenate([high, low, jnp.zeros((12, B), F32)])
        msg[pl.ds(base + 256, 16)] = block.astype(BF16)


def get_tail(msg, base):
    wg = msg[pl.ds(base, 256)].astype(F32)
    block = msg[pl.ds(base + 256, 16)].astype(F32)
    return wg, block[0:2] + block[2:4]


def local(s0, r1, r2, r3, weight, bias, cot, act, msg):
    w = weight[...]
    over_nodes = (((0,), (0,)), ((), ()))
    w_twice = jnp.concatenate([w, w])
    wg, bg = jnp.zeros((2 * B, 256), F32), jnp.zeros((1, 256), F32)
    for k, r in enumerate((None, r3, r2, r1)):
        if k == 0:
            c = cot[...]
        else:
            c = jnp.concatenate([r[1024:1280], r[1280:1536]], axis=1)
        y = s0[pl.ds(k * 256, 256)]
        for d, r in ((1, r1), (2, r2), (3, r3)):
            y += r[pl.ds((k + d) % 4 * 256, 256)].astype(F32)
        y_high = y.astype(BF16)
        y_low = (y - y_high.astype(F32)).astype(BF16)
        y_both = jnp.concatenate([y_high, y_low], axis=1)
        summed = jnp.dot(y_both, w_twice, preferred_element_type=F32)
        pre = summed + bias[...]
        sig = jax.nn.sigmoid(pre)
        if k == 0:
            act[...] = (pre * sig).astype(BF16)
        slope = sig * (1.0 + pre * (1.0 - sig))
        grad = (c.astype(F32) * slope).astype(BF16)
        g = lax.dot_general(w, grad, (((1,), (1,)), ((), ())), preferred_element_type=F32)
        g = g.astype(BF16)
        msg[pl.ds(k * 256, B)] = g[:, 0:B]
        msg[pl.ds(k * 256 + B, B)] = g[:, B : 2 * B]
        wg += lax.dot_general(y_both, grad, over_nodes, preferred_element_type=F32)
        bg += jnp.sum(grad.astype(F32), axis=0, keepdims=True)
    wg = wg[0:B] + wg[B : 2 * B]
    put_tail(
        msg,
        1024,
        jnp.concatenate([wg[:, 0:B], wg[:, B : 2 * B]]),
        jnp.concatenate([bg[:, 0:B], bg[:, B : 2 * B]]),
    )


def sum_tails(pieces):
    wg, bg = get_tail(pieces[0], 1024)
    for piece in pieces[1:]:
        wg_r, bg_r = get_tail(piece, 1024)
        wg += wg_r
        bg += bg_r
    return wg, bg


def backward_tiles(key, places, tab, adj, *refs):
    def product(t, i):
        return jnp.dot(gs[i], t, preferred_element_type=F32)

    pieces, refs, gs = refs[: len(places)], refs[len(places) : -1], refs[-1]
    for place, piece in zip(places, pieces):
        load_blocks([piece], 1024, gs.at[pl.ds(place * 8, 8)])
    if key < 2:
        if key == 0:
            acc, tail = refs
            acc[...] = jnp.zeros((9, B, B), F32)
        else:
            _, tail_in, acc, tail = refs
        each_tile(tab, key, 4, adj, product, acc)
        wg, bg = sum_tails(pieces)
        if key == 1:
            wg, bg = wg + tail_in[0:256], bg + tail_in[256:258]
        put_tail(tail, 0, wg, bg)
        return
    acc_in, tail_in, *outs, acc = refs
    first = 2 if key == 2 else 0
    last = first + 2 * len(outs)
    acc[first:last] = acc_in[first:last]
    each_tile(tab, key, 4, adj, product, acc)
    wg, bg = sum_tails(pieces)
    wg, bg = wg + tail_in[0:256], bg + tail_in[256:258]
    for k, m in enumerate(outs):
        m[0:B] = acc[first + 2 * k].astype(m.dtype)
        m[B : 2 * B] = acc[first + 2 * k + 1].astype(m.dtype)
        put_tail(m, 256, wg, bg)


def last_sum(m0, r1, r2, r3, feat, wgrad, bgrad):
    for k in range(2):
        rows = pl.ds(k * B, B)
        total = m0[rows] + (r1[rows].astype(F32) + r2[rows].astype(F32) + r3[rows].astype(F32))
        feat[rows] = total.T.astype(BF16)
    wg, block = m0[pl.ds(256, 256)], m0[pl.ds(512, 16)]
    bg = block[0:2]
    for r in (r1, r2, r3):
        wg_r, bg_r = get_tail(r, 256)
        wg += wg_r
        bg += bg_r
    wgrad[:, 0:B] = wg[0:B]
    wgrad[:, B : 2 * B] = wg[B : 2 * B]
    bgrad[:, 0:B] = bg[0:1]
    bgrad[:, B : 2 * B] = bg[1:2]


def on_device(
    features, weight, bias_vector, adjacency, tile_rows, tile_cols, tile_count, cotangent
):
    adj = adjacency[0, 0]
    x1, x3, x2 = permute([features] * 3, "row", [row_shift(d) for d in ORDER])
    forward_tab, backward_tab = call(
        sort_tiles,
        (sds(1, TAB, jnp.int32), sds(1, BACKWARD_TAB, jnp.int32)),
        [VMEM] * 3,
    )(tile_rows[0], tile_cols[0], tile_count)
    half = jax.ShapeDtypeStruct((33, B, B), F32)
    tiles, acc0, acc1 = call(
        hold,
        (jax.ShapeDtypeStruct((128, B, B), BF16), half, half),
        [ANY],
        [pltpu.SemaphoreType.DMA((8,))],
        limit=43,
    )(adj)
    xs = (features, x3, x2, x1)
    scratch = [pltpu.VMEM((8, B, B), BF16)]
    _, other = call(
        functools.partial(forward_tiles, 0),
        (half, sds(4096)),
        [SMEM] + [VMEM] * 6,
        scratch,
        tiles=64,
        aliases={6: 0},
    )(forward_tab, *xs, tiles, acc0)
    got = lax.ppermute(other, "col", core_swap())
    acc = call(
        functools.partial(forward_tiles, 1),
        half,
        [SMEM] + [VMEM] * 6,
        scratch,
        aliases={6: 0},
    )(forward_tab, *xs, tiles, acc1)
    ms = call(core_sum, (sds(1024, dtype=F32),) + (sds(1024),) * 3, [VMEM] * 2)(acc, got)
    r2, r1, r3 = permute([ms[d] for d in FAR_FIRST], "col", [col_shift(True, d) for d in FAR_FIRST])
    total, msg = call(first_sum, (sds(1024, dtype=F32), sds(1536)), [VMEM] * 5)(
        ms[0], r1, r2, r3, cotangent
    )
    r2, r1, r3 = permute([msg] * 3, "col", [col_shift(False, d) for d in FAR_FIRST])
    act, msg = call(local, (sds(256, 256), sds(1024 + TAIL)), [VMEM] * 7)(
        total, r1, r2, r3, weight, bias_vector.reshape(1, 256), cotangent
    )
    r1, r3, r2 = permute([msg] * 3, "col", [col_shift(True, d) for d in ORDER], False)
    mine = [msg, r3, r2, r1]
    theirs = [None] * 4
    for k in (0, 3):
        theirs[k] = lax.ppermute(mine[k], "col", core_swap())
    out, tail = sds(256 + TAIL), sds(TAIL, dtype=F32)
    sums = jax.ShapeDtypeStruct((9, B, B), F32)
    blocks, acc = pltpu.VMEM((64, B, B), BF16), pltpu.VMEM((9, B, B), F32)

    def backward(key, places, outs, scratch, tiles, aliases, *extra):
        pieces = [(mine + theirs)[p] for p in places]
        return call(
            functools.partial(backward_tiles, key, places),
            outs,
            [SMEM] + [VMEM] * (1 + len(places) + len(extra)),
            scratch,
            tiles=tiles,
            aliases=aliases,
        )(backward_tab, adj, *pieces, *extra)

    state = backward(0, (0, 3, 4), (sums, tail), [blocks], 48, None)
    mine[1], mine[2], *state = lax.optimization_barrier((mine[1], mine[2], *state))
    for k in (1, 2):
        theirs[k] = lax.ppermute(mine[k], "col", core_swap())
    state = backward(1, (1, 2, 7), (sums, tail), [blocks], 48, {5: 0}, *state)
    ms = backward(2, (5, 6), (out,) * 3, [acc, blocks], 16, None, *state)
    (m,) = backward(3, (5, 6), (sds(256 + TAIL, dtype=F32),), [acc, blocks], 0, None, *state)
    ms = [ms[d - 1] for d in ORDER]
    rs = [lax.ppermute(a, "row", row_shift(d)) for a, d in zip(ms, ORDER)]
    feat, wgrad, bgrad = call(
        last_sum, (sds(256, 128), sds(128, 256, F32), sds(1, 256, F32)), [VMEM] * 4
    )(m, *rs)
    return (act, feat, wgrad, bgrad.reshape(256))


def solution(mesh):
    placed = (
        P(("row", "col"), None),
        P(),
        P(),
        P("row", "col", None, None, None),
        P("row", "col", None),
        P("row", "col", None),
        P("row", "col"),
        P(("row", "col"), None),
    )
    return jax.shard_map(
        on_device,
        mesh=mesh,
        in_specs=placed,
        out_specs=(P(("row", "col"), None), P(("row", "col"), None), P(), P()),
        check_vma=False,
    )
```

```python
import functools

import jax
import jax.numpy as jnp
from jax import lax
from jax.experimental import pallas as pl
from jax.experimental.pallas import tpu as pltpu
from jax.sharding import PartitionSpec as P

F32 = jnp.float32
BF16 = jnp.bfloat16
B = 128
VMEM = pl.BlockSpec(memory_space=pltpu.VMEM)
SMEM = pl.BlockSpec(memory_space=pltpu.SMEM)
ANY = pl.BlockSpec(memory_space=pl.ANY)
TAIL = 272
UNROLL = 16
WIDTH = 144
TAB = 384
BACKWARD_TAB = 640


def at(y, z, core):
    return (y * 4 + z) * 2 + core


def ring_of(y, z, core):
    return (core + y + z) % 2


def col_shift(first, d):
    pairs = []
    for y in range(4):
        for z in range(4):
            for core in range(2):
                ring = ring_of(y, z, core)
                along_z = (ring == 0) == first
                to_y, to_z = (y, (z + d) % 4) if along_z else ((y + d) % 4, z)
                pairs.append((at(y, z, core), at(to_y, to_z, ring_of(to_y, to_z, ring))))
    return pairs


def core_swap():
    return [(c, c ^ 1) for c in range(32)]


def row_shift(d):
    return [(r, (r + d) % 4) for r in range(4)]


def call(kernel, outs, ins, scratch=(), tiles=0, nbytes=0, aliases=None, limit=24):
    return pl.pallas_call(
        kernel,
        out_shape=outs,
        in_specs=ins,
        out_specs=jax.tree.map(lambda _: VMEM, outs),
        scratch_shapes=list(scratch),
        input_output_aliases=aliases or {},
        compiler_params=pltpu.CompilerParams(vmem_limit_bytes=limit * 2**20),
        cost_estimate=pl.CostEstimate(
            flops=2 * tiles * B**3, bytes_accessed=nbytes + tiles * 2**16, transcendentals=0
        ),
    )


def sds(rows, cols=B, dtype=BF16):
    return jax.ShapeDtypeStruct((rows, cols), dtype)


def permute(arrays, axis, pairs, together=True):
    arrays = lax.optimization_barrier(tuple(arrays))
    moved = [lax.ppermute(a, axis, p) for a, p in zip(arrays, pairs)]
    return lax.optimization_barrier(moved) if together else moved


ORDER = (1, 3, 2)
FAR_FIRST = (2, 1, 3)


def sort_tiles(rows, cols, count, forward_tab, backward_tab):
    r, c = lax.axis_index("row"), lax.axis_index("col")
    core, z, y = c % 2, (c // 2) % 4, c // 8
    rows, cols = rows[...], cols[...]
    owner, sub = rows // 2, rows % 2
    core_to, z_to, y_to = owner % 2, (owner // 2) % 4, owner // 8
    dz, dy = (z_to - z + 4) % 4, (y_to - y + 4) % 4
    ring_to = ring_of(y_to, z_to, core_to)
    first = jnp.where(ring_to == 0, dz, dy)
    second = jnp.where(ring_to == 0, dy, dz)
    pos = (first * 4 + second) * 2 + sub
    half = (ring_to != ring_of(y, z, core)).astype(jnp.int32)
    ahead = (cols // 2 - r + 4) % 4
    slot = lax.broadcasted_iota(jnp.int32, (1, 128), 1)

    def table(key, keys, take, to, pad, width):
        key = jnp.where(slot < count[...], key, keys)
        is_key = [jnp.where(key == k, 1.0, 0.0) for k in range(keys)]
        is_key = jnp.concatenate(is_key + [jnp.zeros((8 - keys, 128), F32)]).astype(BF16)
        low = lax.broadcasted_iota(jnp.int32, (128, 128), 0)
        high = lax.broadcasted_iota(jnp.int32, (128, 128), 1)
        before = jnp.where(low < high, 1.0, 0.0).astype(BF16)
        rank = jnp.dot(is_key, before, preferred_element_type=F32)
        place = jnp.full((1, 128), -1.0, F32)
        for k in range(keys):
            place = jnp.where(key == k, rank[k : k + 1] + float(k * WIDTH), place)
        place = jnp.broadcast_to(place, (8, 128)).T[:, 0:1].astype(jnp.int32)
        spots = lax.broadcasted_iota(jnp.int32, (128, width), 1)
        at_spot = jnp.where(place == spots, 1.0, 0.0).astype(BF16)
        fields = [slot.astype(F32), take.astype(F32), to.astype(F32), jnp.ones((1, 128), F32)]
        fields = jnp.concatenate(fields + [jnp.zeros((4, 128), F32)]).astype(BF16)
        found = jnp.dot(fields, at_spot, preferred_element_type=F32).astype(jnp.int32)
        entry = found[0:1] + found[1:2] * 2**8 + found[2:3] * 2**16
        entry = jnp.where(found[3:4] > 0, entry, pad * 2**16)
        total = jnp.sum(is_key.astype(F32), axis=1, keepdims=True).astype(jnp.int32)
        for k in range(keys):
            groups = (total[k : k + 1] + (UNROLL - 1)) // UNROLL
            entry = jnp.where(spots[0:1] == keys * WIDTH + k, groups, entry)
        return entry

    forward_tab[...] = table(1 - half, 2, ahead * 2 + cols % 2, pos, 32, TAB)
    late = ((first == 1) | (first == 2)).astype(jnp.int32)
    group = late + jnp.where(first == 0, 0, half)
    key = jnp.where(group < 2, group, jnp.where(ahead == 0, 3, 2))
    take = half * 32 + pos
    backward_tab[...] = table(key, 4, take, ahead * 2 + cols % 2, 8, BACKWARD_TAB)


def hold(adj, tiles, acc0, acc1, sem):
    n = sem.shape[0]
    parts = [pl.ds(k * (128 // n), 128 // n) for k in range(n)]
    copies = [
        pltpu.make_async_copy(adj.at[part], tiles.at[part], sem.at[k])
        for k, part in enumerate(parts)
    ]
    for copy in copies:
        copy.start()

    def block(i, _):
        acc0[i] = jnp.zeros((B, B), F32)
        acc1[i] = jnp.zeros((B, B), F32)
        return 0

    lax.fori_loop(0, 32, block, 0, unroll=4)
    for copy in copies:
        copy.wait()


def each_tile(tab, key, keys, adj, product, acc):
    def body(g, _):
        parts = []
        for u in range(UNROLL):
            e = tab[0, key * WIDTH + g * UNROLL + u]
            parts.append((product(adj[e & 127], (e >> 8) & 63), e >> 16))
        for part, to in parts:
            acc[to] += part
        return 0

    lax.fori_loop(0, tab[0, keys * WIDTH + key], body, 0)


def load_blocks(refs, rows, to):
    for k, ref in enumerate(refs):
        for i in range(rows // B):
            to[k * (rows // B) + i] = ref[i * B : (i + 1) * B]


def forward_tiles(key, tab, x0, x1, x2, x3, adj, _, acc, *refs):
    *out, xs = refs
    load_blocks([x0, x1, x2, x3], 256, xs)
    each_tile(tab, key, 2, adj, lambda t, i: jnp.dot(t, xs[i], preferred_element_type=F32), acc)
    if key == 0:

        def store(i, _):
            out[0][pl.ds(pl.multiple_of(i * B, B), B)] = acc[i].astype(BF16)
            return 0

        lax.fori_loop(0, 32, store, 0, unroll=4)


def core_sum(acc, got, m0, m1, m2, m3):
    for k, m in enumerate((m0, m1, m2, m3)):
        for i in range(8):
            rows = pl.ds((k * 8 + i) * B, B)
            total = acc[k * 8 + i] + got[rows].astype(F32)
            m[i * B : (i + 1) * B] = total.astype(m.dtype)


def first_sum(m0, r1, r2, r3, cot, total, msg):
    for i in range(0, 1024, 256):
        rows = pl.ds(i, 256)
        t = m0[rows] + (r1[rows].astype(F32) + r2[rows].astype(F32) + r3[rows].astype(F32))
        total[rows] = t
        msg[rows] = t.astype(BF16)
    msg[1024:1280] = cot[:, 0:B]
    msg[1280:1536] = cot[:, B : 2 * B]


def put_tail(msg, base, wg, bg):
    msg[pl.ds(base, 256)] = wg.astype(msg.dtype)
    if msg.dtype == F32:
        msg[pl.ds(base + 256, 16)] = jnp.concatenate([bg, jnp.zeros((14, B), F32)])
    else:
        high = bg.astype(BF16).astype(F32)
        low = bg - high
        block = jnp.concatenate([high, low, jnp.zeros((12, B), F32)])
        msg[pl.ds(base + 256, 16)] = block.astype(BF16)


def get_tail(msg, base):
    wg = msg[pl.ds(base, 256)].astype(F32)
    block = msg[pl.ds(base + 256, 16)].astype(F32)
    return wg, block[0:2] + block[2:4]


def local(s0, r1, r2, r3, weight, bias, cot, act, msg):
    w = weight[...]
    over_nodes = (((0,), (0,)), ((), ()))
    wg, bg = jnp.zeros((B, 256), F32), jnp.zeros((1, 256), F32)
    for k, r in enumerate((None, r3, r2, r1)):
        if k == 0:
            c = cot[...]
        else:
            c = jnp.concatenate([r[1024:1280], r[1280:1536]], axis=1)
        y = s0[pl.ds(k * 256, 256)]
        for d, r in ((1, r1), (2, r2), (3, r3)):
            y += r[pl.ds((k + d) % 4 * 256, 256)].astype(F32)
        y_high = y.astype(BF16)
        y_low = (y - y_high.astype(F32)).astype(BF16)
        summed = jnp.dot(y_high, w, preferred_element_type=F32) + jnp.dot(
            y_low, w, preferred_element_type=F32
        )
        pre = summed + bias[...]
        sig = jax.nn.sigmoid(pre)
        if k == 0:
            act[...] = (pre * sig).astype(BF16)
        slope = sig * (1.0 + pre * (1.0 - sig))
        grad = (c.astype(F32) * slope).astype(BF16)
        g = lax.dot_general(w, grad, (((1,), (1,)), ((), ())), preferred_element_type=F32)
        g = g.astype(BF16)
        msg[pl.ds(k * 256, B)] = g[:, 0:B]
        msg[pl.ds(k * 256 + B, B)] = g[:, B : 2 * B]
        wg += lax.dot_general(y_high, grad, over_nodes, preferred_element_type=F32)
        wg += lax.dot_general(y_low, grad, over_nodes, preferred_element_type=F32)
        bg += jnp.sum(grad.astype(F32), axis=0, keepdims=True)
    put_tail(
        msg,
        1024,
        jnp.concatenate([wg[:, 0:B], wg[:, B : 2 * B]]),
        jnp.concatenate([bg[:, 0:B], bg[:, B : 2 * B]]),
    )


def sum_tails(pieces):
    wg, bg = get_tail(pieces[0], 1024)
    for piece in pieces[1:]:
        wg_r, bg_r = get_tail(piece, 1024)
        wg += wg_r
        bg += bg_r
    return wg, bg


def backward_tiles(key, places, tab, adj, *refs):
    def product(t, i):
        return jnp.dot(gs[i], t, preferred_element_type=F32)

    pieces, refs, gs = refs[: len(places)], refs[len(places) : -1], refs[-1]
    for place, piece in zip(places, pieces):
        load_blocks([piece], 1024, gs.at[pl.ds(place * 8, 8)])
    if key < 2:
        if key == 0:
            acc, tail = refs
            acc[...] = jnp.zeros((9, B, B), F32)
        else:
            _, tail_in, acc, tail = refs
        each_tile(tab, key, 4, adj, product, acc)
        wg, bg = sum_tails(pieces)
        if key == 1:
            wg, bg = wg + tail_in[0:256], bg + tail_in[256:258]
        put_tail(tail, 0, wg, bg)
        return
    acc_in, tail_in, *outs, acc = refs
    first = 2 if key == 2 else 0
    last = first + 2 * len(outs)
    acc[first:last] = acc_in[first:last]
    each_tile(tab, key, 4, adj, product, acc)
    wg, bg = sum_tails(pieces)
    wg, bg = wg + tail_in[0:256], bg + tail_in[256:258]
    for k, m in enumerate(outs):
        m[0:B] = acc[first + 2 * k].astype(m.dtype)
        m[B : 2 * B] = acc[first + 2 * k + 1].astype(m.dtype)
        put_tail(m, 256, wg, bg)


def last_sum(m0, r1, r2, r3, feat, wgrad, bgrad):
    for k in range(2):
        rows = pl.ds(k * B, B)
        total = m0[rows] + (r1[rows].astype(F32) + r2[rows].astype(F32) + r3[rows].astype(F32))
        feat[rows] = total.T.astype(BF16)
    wg, block = m0[pl.ds(256, 256)], m0[pl.ds(512, 16)]
    bg = block[0:2]
    for r in (r1, r2, r3):
        wg_r, bg_r = get_tail(r, 256)
        wg += wg_r
        bg += bg_r
    wgrad[:, 0:B] = wg[0:B]
    wgrad[:, B : 2 * B] = wg[B : 2 * B]
    bgrad[:, 0:B] = bg[0:1]
    bgrad[:, B : 2 * B] = bg[1:2]


def on_device(
    features, weight, bias_vector, adjacency, tile_rows, tile_cols, tile_count, cotangent
):
    adj = adjacency[0, 0]
    x1, x3, x2 = permute([features] * 3, "row", [row_shift(d) for d in ORDER])
    forward_tab, backward_tab = call(
        sort_tiles,
        (sds(1, TAB, jnp.int32), sds(1, BACKWARD_TAB, jnp.int32)),
        [VMEM] * 3,
    )(tile_rows[0], tile_cols[0], tile_count)
    half = jax.ShapeDtypeStruct((33, B, B), F32)
    tiles, acc0, acc1 = call(
        hold,
        (jax.ShapeDtypeStruct((128, B, B), BF16), half, half),
        [ANY],
        [pltpu.SemaphoreType.DMA((8,))],
        limit=43,
    )(adj)
    xs = (features, x3, x2, x1)
    scratch = [pltpu.VMEM((8, B, B), BF16)]
    _, other = call(
        functools.partial(forward_tiles, 0),
        (half, sds(4096)),
        [SMEM] + [VMEM] * 6,
        scratch,
        tiles=64,
        aliases={6: 0},
    )(forward_tab, *xs, tiles, acc0)
    got = lax.ppermute(other, "col", core_swap())
    acc = call(
        functools.partial(forward_tiles, 1),
        half,
        [SMEM] + [VMEM] * 6,
        scratch,
        aliases={6: 0},
    )(forward_tab, *xs, tiles, acc1)
    ms = call(core_sum, (sds(1024, dtype=F32),) + (sds(1024),) * 3, [VMEM] * 2)(acc, got)
    r2, r1, r3 = permute([ms[d] for d in FAR_FIRST], "col", [col_shift(True, d) for d in FAR_FIRST])
    total, msg = call(first_sum, (sds(1024, dtype=F32), sds(1536)), [VMEM] * 5)(
        ms[0], r1, r2, r3, cotangent
    )
    r1, r3, r2 = permute([msg] * 3, "col", [col_shift(False, d) for d in ORDER])
    act, msg = call(local, (sds(256, 256), sds(1024 + TAIL)), [VMEM] * 7)(
        total, r1, r2, r3, weight, bias_vector.reshape(1, 256), cotangent
    )
    r1, r3, r2 = permute([msg] * 3, "col", [col_shift(True, d) for d in ORDER], False)
    mine = [msg, r3, r2, r1]
    theirs = [None] * 4
    for k in (0, 3):
        theirs[k] = lax.ppermute(mine[k], "col", core_swap())
    out, tail = sds(256 + TAIL), sds(TAIL, dtype=F32)
    sums = jax.ShapeDtypeStruct((9, B, B), F32)
    blocks, acc = pltpu.VMEM((64, B, B), BF16), pltpu.VMEM((9, B, B), F32)

    def backward(key, places, outs, scratch, tiles, aliases, *extra):
        pieces = [(mine + theirs)[p] for p in places]
        return call(
            functools.partial(backward_tiles, key, places),
            outs,
            [SMEM] + [VMEM] * (1 + len(places) + len(extra)),
            scratch,
            tiles=tiles,
            aliases=aliases,
        )(backward_tab, adj, *pieces, *extra)

    state = backward(0, (0, 3, 4), (sums, tail), [blocks], 48, None)
    mine[1], mine[2], *state = lax.optimization_barrier((mine[1], mine[2], *state))
    for k in (1, 2):
        theirs[k] = lax.ppermute(mine[k], "col", core_swap())
    state = backward(1, (1, 2, 7), (sums, tail), [blocks], 48, {5: 0}, *state)
    ms = backward(2, (5, 6), (out,) * 3, [acc, blocks], 16, None, *state)
    (m,) = backward(3, (5, 6), (sds(256 + TAIL, dtype=F32),), [acc, blocks], 0, None, *state)
    ms = [ms[d - 1] for d in ORDER]
    rs = [lax.ppermute(a, "row", row_shift(d)) for a, d in zip(ms, ORDER)]
    feat, wgrad, bgrad = call(
        last_sum, (sds(256, 128), sds(128, 256, F32), sds(1, 256, F32)), [VMEM] * 4
    )(m, *rs)
    return (act, feat, wgrad, bgrad.reshape(256))


def solution(mesh):
    placed = (
        P(("row", "col"), None),
        P(),
        P(),
        P("row", "col", None, None, None),
        P("row", "col", None),
        P("row", "col", None),
        P("row", "col"),
        P(("row", "col"), None),
    )
    return jax.shard_map(
        on_device,
        mesh=mesh,
        in_specs=placed,
        out_specs=(P(("row", "col"), None), P(("row", "col"), None), P(), P()),
        check_vma=False,
    )
```
